128 devices in a mesh: attn: 16 (over z, x), expert: 8 (over y, core).
Axes of the slice: x: 4, y: 4, z: 4, core: 2. Of those that a mesh axis runs over, the one named last changes fastest.
Arguments:
- residual: bfloat16 [512, 6144], P('attn'), may hold values from -90 to 90
- queries: bfloat16 [512, 6144], P('attn', 'expert'), may hold values from -100 to 100
- new_keys: bfloat16 [512, 1024], P('attn', 'expert'), may hold values from -4 to 4
- new_values: bfloat16 [512, 1024], P('attn', 'expert'), may hold values from -4 to 4
- key_cache: bfloat16 [512, 8, 320, 128], P('attn', 'expert'), may hold values from -4 to 4
- value_cache: bfloat16 [512, 8, 320, 128], P('attn', 'expert'), may hold values from -4 to 4
- cache_lengths: int32 [512], P('attn'), may hold values from 1 to 320, 81920 in all
- out_weight: bfloat16 [6144, 6144], P('expert'), may hold values from -0.109375 to 0.109375
- norm_gain: float32 [6144], replicated, may hold values from 0.1 to 1.9
- gate_weight: bfloat16 [6144, 49152], P(None, ('attn', 'expert')), may hold values from -0.078125 to 0.078125
- up_weight: bfloat16 [6144, 49152], P(None, ('attn', 'expert')), may hold values from -0.078125 to 0.078125
- down_weight: bfloat16 [49152, 6144], P(('attn', 'expert')), may hold values from -0.21875 to 0.21875
- routes: int32 [512, 2], P('attn'), may hold values from 0 to 3, all different within a row; in each aligned block of 32 rows (0 to 31, 32 to 63, ...) at most 24 rows name the same one
- route_gates: float32 [512, 2], P('attn'), may hold values from 0.2 to 1
Outputs:
- layer_out: float32 [512, 6144], P('attn', 'expert')
The draws below stay inside these ranges and needn't reach their ends.
Inputs may be any that keep to these rules, and one draw needn't show every extreme that they name: Positions from cache_lengths[b] on are not part of sequence b's cache; some sequence fills all 320 positions. `routes`: the two experts of a row differ. Among the 32 rows of one attn index no expert is named more than 24 times, a bound that some block reaches in the rows of some attn index.
All inputs are finite; a program needn't handle non-finite values. No bound on the sum of `cache_lengths` on one device may be relied on, other than what follows from the above.
Results may differ from the reference program's by a relative error of at most 0.003.
Values may be sent and summed in bfloat16 or wider, within the bound.
No kernel may reach another device: no remote copies, remote signals or barrier semaphores. Data moves between devices by JAX's collectives and lax.ppermute only.
A program may use at most 128 MiB of HBM per device.

```python
import math
import jax
import jax.numpy as jnp
import numpy as np
from jax import lax

D = 6144
H = 48
KVH = 8
HD = 128
EXPERTS = 4
FF = 12288
B_DEV = 32
LMAX = 320
CAP = 24
B = 512


def cache_base(key):
    return jnp.clip(jax.random.normal(key, (B, KVH, LMAX, HD), jnp.float32), -4.0, 4.0)


def draw_key_cache(key, part):
    shared = cache_base(key)
    return shared.astype(jnp.bfloat16)


def draw_queries(key, part):
    key = jax.random.fold_in(key, 2)
    values = jnp.clip(jax.random.normal(key, (B, H * HD), jnp.float32), -4.0, 4.0)
    return values.astype(jnp.bfloat16)


def draw_new_keys(key, part):
    key = jax.random.fold_in(key, 3)
    values = jnp.clip(jax.random.normal(key, (B, KVH * HD), jnp.float32), -4.0, 4.0)
    return values.astype(jnp.bfloat16)


def draw_residual(key, part):
    key = jax.random.fold_in(key, 4)
    key_rows, key_cols, key_base = jax.random.split(key, 3)
    rising = 3.0 ** (jnp.arange(D).astype(jnp.float32) / (D - 1))
    row_scale = 0.2 * jnp.exp(jax.random.uniform(key_rows, (B, 1), jnp.float32, 0.0, jnp.log(10.0)))
    col_scale = 0.2 * jnp.exp(jax.random.uniform(key_cols, (1, D), jnp.float32, 0.0, jnp.log(10.0))) * rising[None, :]
    values = jnp.clip(jax.random.normal(key_base, (B, D), jnp.float32), -4.0, 4.0)
    return (values * row_scale * col_scale).astype(jnp.bfloat16)


def with_spikes(entries, key, source, target, blocks, factor):
    owner, partner = [(jnp.arange(entries.shape[dim]) // (entries.shape[dim] // blocks)).reshape([-1 if axis == dim else 1 for axis in range(entries.ndim)]) for dim in (source, target)]
    chosen = jax.random.permutation(key, blocks)[partner]
    strong = (owner == chosen) | (owner == (partner + blocks // 2) % blocks)
    return jnp.where(strong, factor * entries, entries)


def level_of(own_key, shape, shards, low, top_value):
    level, own = 1.0, jax.random.fold_in(own_key, 6)
    for dim, blocks in shards:
        steps = jnp.exp(jax.random.uniform(jax.random.fold_in(own, dim), (blocks,), jnp.float32, low / len(shards), top_value / len(shards)))
        level = level * jnp.repeat(steps, shape[dim] // blocks).reshape([-1 if axis == dim else 1 for axis in range(len(shape))])
    return level


def length_profile(number_of, total, most, slope):
    loads = [(1 << 20) // math.isqrt(rank ** slope) + 1 for rank in range(2, number_of + 1)]
    surplus, given = total - most - (number_of - 1), [1] * (number_of - 1)
    while surplus > 0:
        candidates = [i for i in range(number_of - 1) if given[i] < most]
        whole, budget = sum([loads[i] for i in candidates]), surplus
        for i in candidates:
            more = min(most - given[i], max(1, budget * loads[i] // whole), surplus)
            given[i] = given[i] + more
            surplus = surplus - more
    return np.array([most] + given)


def uneven(rng, number_of, total, bound, slope):
    if number_of == 2:
        one = jax.random.randint(rng, (), max(1, total - bound), min(bound, total - 1) + 1)
        return jnp.stack([one, total - one])
    sizes = jnp.asarray(length_profile(number_of, total, bound, slope), jnp.int32)
    twos = (number_of - 1) // 2
    source_of, taker = sizes[1:1 + 2 * twos:2], sizes[2:2 + 2 * twos:2]
    slack = jnp.minimum(source_of - 1, bound - taker)
    passed = jax.random.randint(jax.random.fold_in(rng, 1), (twos,), 0, 1 << 20) % (slack + 1)
    sizes = sizes.at[1:1 + 2 * twos:2].set(source_of - passed).at[2:2 + 2 * twos:2].set(taker + passed)
    return sizes[jax.random.permutation(jax.random.fold_in(rng, 2), number_of)]


def deal_out(stream_key, own, number, rows, number_of, top, reach, skew):
    order = jax.random.permutation(stream_key, number_of)
    heavy_load, common = shares(number_of, rows * top, reach, skew, True), shares(number_of, rows * top, reach, skew, False)
    places = jnp.arange(number_of)

    def named(tallies, rotation):
        used = int((tallies > 0).sum())
        fixed = max(1, used // 4)
        shifted = fixed + (places - fixed + rotation * (used - fixed)) % max(1, number_of - fixed)
        return jnp.zeros((number_of,), jnp.int32).at[order[jnp.where(places < fixed, places, shifted)]].set(jnp.asarray(tallies, jnp.int32))

    tallies = jnp.where(number % 4 == 0, named(heavy_load, number // 4), named(common, number - number // 4 - 1))
    mixed = jax.random.permutation(jax.random.fold_in(own, 3), number_of)
    donor, taker = mixed[0:number_of // 2 * 2:2], mixed[1:number_of // 2 * 2:2]
    slack = jnp.minimum(tallies[donor] - 1, reach - tallies[taker]) // 2
    slack = jnp.where((donor == order[0]) | (taker == order[0]) | (tallies[taker] == 0), 0, jnp.maximum(slack, 0))
    shifted = jax.random.randint(jax.random.fold_in(own, 4), (number_of // 2,), 0, 1 << 20) % (slack + 1)
    tallies = tallies.at[donor].add(-shifted).at[taker].add(shifted)
    items = jnp.searchsorted(jnp.cumsum(tallies), jnp.arange(rows * top), side="right").astype(jnp.int32)
    listing = items.reshape(top, rows).T
    listing = listing[jax.random.permutation(jax.random.fold_in(own, 1), rows)]
    rotation = jax.random.randint(jax.random.fold_in(own, 2), (rows, 1), 0, top)
    return jnp.take_along_axis(listing, (jnp.arange(top)[None, :] + rotation) % top, axis=1)


def shares(amount, total, bound, slope, full):
    loads = [(1 << 20) // math.isqrt(standing ** slope) + 1 for standing in range(1, amount + 1)]
    largest = bound if full else min(bound, max(-(-total // amount), total * loads[0] // sum(loads)))
    least = 1 if total - largest >= amount - 1 else 0
    counts, spare = [largest] + [least] * (amount - 1), total - largest - least * (amount - 1)
    while spare > 0:
        free = [i for i in range(1, amount) if counts[i] < largest] or [i for i in range(1, amount) if counts[i] < bound]
        pool, left = sum([loads[i] for i in free]), spare
        for i in free:
            extra = min(bound - counts[i], max(1, left * loads[i] // pool), spare)
            counts[i] = counts[i] + extra
            spare = spare - extra
    return np.array(counts)


def centred(own_key, shape, deviation, most, cuts=(), dtype=jnp.bfloat16):
    result = deviation * jax.random.normal(own_key, shape, jnp.float32)
    if cuts:
        result = result * level_of(own_key, shape, cuts, -0.22, 0.18)
    return jnp.clip(result, -most, most).astype(dtype)


def bell_draw_with(own_key, shape, deviation, most, shards, heavy, held_as=jnp.bfloat16):
    array = deviation * jax.random.normal(own_key, shape, jnp.float32)
    if shards:
        array = array * level_of(own_key, shape, shards, -0.22, 0.18)
    return jnp.clip(with_spikes(array, jax.random.fold_in(own_key, 3), *heavy), -most, most).astype(held_as)


def setup_inputs(seed: int = 0) -> dict:
    seeds = jax.random.split(jax.random.key(seed), 15)
    residual = draw_residual(jax.random.fold_in(seeds[14], 71), 0)
    queries = draw_queries(jax.random.fold_in(seeds[14], 71), 0)
    new_keys = draw_new_keys(jax.random.fold_in(seeds[14], 71), 0)
    new_values = centred(seeds[3], (B, KVH * HD), 1.0, 4.0, ((0, 16), (1, 8)))
    key_cache = draw_key_cache(jax.random.fold_in(seeds[14], 71), 0)
    value_cache = centred(seeds[5], (B, KVH, LMAX, HD), 1.0, 4.0, ((0, 16), (1, 8)))
    cache_lengths = uneven(seeds[6], B, B * LMAX // 2, LMAX, 2).astype(jnp.int32)
    out_weight = bell_draw_with(seeds[7], (H * HD, D), (H * HD) ** -0.5, 0.109375, ((0, 8),), (0, 1, 8, 2.0))
    norm_gain = jnp.clip(1.0 + 0.18 * jax.random.normal(seeds[8], (D,), jnp.float32), 0.1, 1.9)
    gate_weight = centred(seeds[9], (D, EXPERTS * FF), D ** -0.5, 0.078125, ((1, 128),))
    up_weight = centred(seeds[10], (D, EXPERTS * FF), D ** -0.5, 0.078125, ((1, 128),))
    down_weight = bell_draw_with(seeds[11], (EXPERTS * FF, D), FF ** -0.5, 0.21875, ((0, 128),), (0, 1, 128, 5.5))
    routes_keys = jax.random.split(jax.random.fold_in(seeds[12], 1), B // B_DEV)
    routes_turns = jax.random.permutation(jax.random.fold_in(seeds[12], 3), B // B_DEV)
    routes = jax.vmap(lambda own, number: deal_out(jax.random.fold_in(seeds[12], 2), own, number, B_DEV, EXPERTS, 2, CAP, 2))(routes_keys, routes_turns).reshape((B, 2))
    route_gates = jnp.clip(0.2 + 0.8 * jax.random.uniform(seeds[13], (B, 2), jnp.float32) ** level_of(seeds[13], (B, 2), ((0, 16),), -0.2, 0.2), 0.2, 1.0)
    return {"residual": residual, "queries": queries, "new_keys": new_keys, "new_values": new_values, "key_cache": key_cache, "value_cache": value_cache, "cache_lengths": cache_lengths, "out_weight": out_weight, "norm_gain": norm_gain, "gate_weight": gate_weight, "up_weight": up_weight, "down_weight": down_weight, "routes": routes, "route_gates": route_gates}


epsilon = 1e-05

def attend_ref(queries, new_keys, new_values, key_cache, value_cache, cache_lengths):
    row_count, kv_groups, cache_span, head_width = key_cache.shape
    heads_per = queries.shape[1] // (kv_groups * head_width)
    score_scale = 1.0 / head_width ** 0.5
    query_heads = queries.astype(jnp.float32).reshape(row_count, kv_groups, heads_per, head_width)
    scores = jnp.einsum('bghd,bgld->bghl', query_heads, key_cache.astype(jnp.float32)) * score_scale
    fresh_scores = jnp.einsum('bghd,bgd->bgh', query_heads, new_keys.astype(jnp.float32).reshape(row_count, kv_groups, head_width)) * score_scale
    visible = (jnp.arange(cache_span)[None, :] < cache_lengths[:, None])[:, None, None, :]
    scores = jnp.where(visible, scores, -jnp.inf)
    largest = jnp.maximum(lax.optimization_barrier(jnp.max(scores, axis=3)), fresh_scores)
    exp_scores = jnp.exp(scores - largest[..., None])
    exp_fresh = jnp.exp(fresh_scores - largest)
    denominator = lax.optimization_barrier(jnp.sum(exp_scores, axis=3)) + exp_fresh
    weights = (exp_scores / denominator[..., None]).astype(jnp.bfloat16)
    weights_new = (exp_fresh / denominator).astype(jnp.bfloat16)
    mixture = jnp.einsum('bghl,bgld->bghd', weights.astype(jnp.float32), value_cache.astype(jnp.float32))
    mixture = mixture + weights_new.astype(jnp.float32)[..., None] * new_values.astype(jnp.float32).reshape(row_count, kv_groups, 1, head_width)
    return mixture.reshape(row_count, kv_groups * heads_per * head_width).astype(jnp.bfloat16)

def reference(residual, queries, new_keys, new_values, key_cache, value_cache, cache_lengths, out_weight, norm_gain, gate_weight, up_weight, down_weight, routes, route_gates):
    attended = attend_ref(queries, new_keys, new_values, key_cache, value_cache, cache_lengths)
    middle = residual.astype(jnp.float32) + jnp.dot(attended, out_weight, preferred_element_type=jnp.float32)
    normed = (middle * lax.rsqrt(lax.optimization_barrier(jnp.mean(middle * middle, axis=1, keepdims=True)) + epsilon) * norm_gain).astype(jnp.bfloat16)
    expert_ids = jnp.arange(EXPERTS)
    coef = lax.optimization_barrier(jnp.sum(route_gates[:, :, None] * (routes[:, :, None] == expert_ids[None, None, :]).astype(jnp.float32), axis=1))

    def add_expert(index, running):
        offset = (index * FF).astype(jnp.int32)
        gate_cols = lax.dynamic_slice_in_dim(gate_weight, offset, FF, 1)
        up_cols = lax.dynamic_slice_in_dim(up_weight, offset, FF, 1)
        down_rows = lax.dynamic_slice_in_dim(down_weight, offset, FF, 0)
        gate_sum = jnp.dot(normed, gate_cols, preferred_element_type=jnp.float32)
        up_sum = jnp.dot(normed, up_cols, preferred_element_type=jnp.float32)
        hidden = (jax.nn.silu(gate_sum) * up_sum).astype(jnp.bfloat16)
        produced = jnp.dot(hidden, down_rows, preferred_element_type=jnp.float32)
        factor = lax.dynamic_slice_in_dim(coef, index.astype(jnp.int32), 1, 1)
        return running + factor * produced
    expert_mix = lax.fori_loop(0, EXPERTS, add_expert, jnp.zeros(middle.shape, jnp.float32))
    return middle + expert_mix
```

```python
import functools
import math

import jax
import jax.numpy as jnp
from jax import lax
from jax.experimental import pallas as pl
from jax.experimental.pallas import tpu as pltpu
from jax.sharding import Mesh, PartitionSpec as P

EXPERTS = 4
CAP = 24
CORES = 2
EPSILON = 1e-05

CHIPS = ("z", "x", "y")
GROUP = ("y", "core")


def attend(queries, new_keys, new_values, key_cache, value_cache, cache_lengths):
    row_count, kv_groups, cache_span, head_width = key_cache.shape
    heads_per = queries.shape[1] // (kv_groups * head_width)
    score_scale = 1.0 / math.sqrt(head_width)
    query_heads = queries.reshape(row_count, kv_groups, heads_per, head_width)
    scores = (
        jnp.einsum("bghd,bgld->bghl", query_heads, key_cache, preferred_element_type=jnp.float32)
        * score_scale
    )
    fresh_scores = (
        jnp.einsum(
            "bghd,bgd->bgh",
            query_heads,
            new_keys.reshape(row_count, kv_groups, head_width),
            preferred_element_type=jnp.float32,
        )
        * score_scale
    )
    visible = (jnp.arange(cache_span)[None, :] < cache_lengths[:, None])[:, None, None, :]
    scores = jnp.where(visible, scores, -jnp.inf)
    largest = jnp.maximum(jnp.max(scores, axis=3), fresh_scores)
    exp_scores = jnp.exp(scores - largest[..., None])
    exp_fresh = jnp.exp(fresh_scores - largest)
    denominator = jnp.sum(exp_scores, axis=3) + exp_fresh
    weights = (exp_scores / denominator[..., None]).astype(jnp.bfloat16)
    weights_new = (exp_fresh / denominator).astype(jnp.bfloat16)
    mixture = jnp.einsum(
        "bghl,bgld->bghd", weights, value_cache, preferred_element_type=jnp.float32
    )
    mixture = mixture + weights_new.astype(jnp.float32)[..., None] * new_values.reshape(
        row_count, kv_groups, 1, head_width
    ).astype(jnp.float32)
    return mixture.reshape(row_count, kv_groups * heads_per * head_width).astype(jnp.bfloat16)


def hidden_kernel(
    core, own, other, gain, gate, up, down, hidden_ref, send_ref, gate_acc, up_acc, squares, hidden
):
    step = pl.program_id(0)
    blocks, cap, width = own.shape[0], own.shape[2], own.shape[3]
    rows = blocks * cap

    @pl.when(step == 0)
    def _():
        gate_acc[...] = jnp.zeros_like(gate_acc)
        up_acc[...] = jnp.zeros_like(up_acc)
        squares[...] = jnp.zeros_like(squares)

    def add_block(source):
        wide = source[...].astype(jnp.float32).reshape(rows, width)
        plain = wide * (1.0 / gain[0])
        squares[...] += jnp.sum(plain * plain, axis=1, keepdims=True)
        block = wide.astype(jnp.bfloat16)
        gate_acc[...] += jnp.dot(block, gate[...], preferred_element_type=jnp.float32)
        up_acc[...] += jnp.dot(block, up[...], preferred_element_type=jnp.float32)

    @pl.when(step < 4)
    def _():
        add_block(own)

    @pl.when((step >= 4) & (step < 8))
    def _():
        add_block(other)

    @pl.when(step == 7)
    def _():
        scale = lax.rsqrt(squares[...] * (1.0 / (8 * width)) + EPSILON)
        gate_sum = gate_acc[...] * scale
        value = (gate_sum / (1.0 + jnp.exp(-gate_sum)) * (up_acc[...] * scale)).astype(jnp.bfloat16)
        hidden[...] = value
        hidden_ref[...] = value

    @pl.when(step >= 8)
    def _():
        out = jnp.dot(hidden[...], down[...], preferred_element_type=jnp.float32)
        send_ref[...] = out.reshape(blocks, 1, cap, width).astype(send_ref.dtype)


def own_kernel(core, hidden, down, out_ref):
    blocks, _, cap, width = out_ref.shape
    out = jnp.dot(hidden[...], down[...], preferred_element_type=jnp.float32)
    out_ref[...] = out.reshape(blocks, 1, cap, width).astype(out_ref.dtype)


def expert_halves(core, own, other, gain, gate, up, down):
    blocks, ys, cap, width = own.shape
    units = gate.shape[1]
    rows = blocks * cap

    def k_block(step, core):
        k = jnp.minimum(step, 7)
        return jnp.where(k < 4, 2 * k + core[0], 2 * (k - 4) + 1 - core[0])

    def n_block(step, core):
        return 2 * jnp.maximum(step - 8, 0) + 1 - core[0]

    return pl.pallas_call(
        hidden_kernel,
        grid_spec=pltpu.PrefetchScalarGridSpec(
            num_scalar_prefetch=1,
            grid=(12,),
            in_specs=[
                pl.BlockSpec((blocks, 1, cap, width), lambda i, c: (0, jnp.minimum(i, 3), 0, 0)),
                pl.BlockSpec((blocks, 1, cap, width), lambda i, c: (0, jnp.clip(i - 4, 0, 3), 0, 0)),
                pl.BlockSpec((1, 1, width), lambda i, c: (k_block(i, c), 0, 0)),
                pl.BlockSpec((width, units), lambda i, c: (k_block(i, c), 0)),
                pl.BlockSpec((width, units), lambda i, c: (k_block(i, c), 0)),
                pl.BlockSpec((units, width), lambda i, c: (0, n_block(i, c))),
            ],
            out_specs=[
                pl.BlockSpec((rows, units), lambda i, c: (0, 0)),
                pl.BlockSpec((blocks, 1, cap, width), lambda i, c: (0, jnp.maximum(i - 8, 0), 0, 0)),
            ],
            scratch_shapes=[
                pltpu.VMEM((rows, units), jnp.float32),
                pltpu.VMEM((rows, units), jnp.float32),
                pltpu.VMEM((rows, 1), jnp.float32),
                pltpu.VMEM((rows, units), jnp.bfloat16),
            ],
        ),
        out_shape=[
            jax.ShapeDtypeStruct((rows, units), jnp.bfloat16),
            jax.ShapeDtypeStruct((blocks, ys, cap, width), jnp.bfloat16),
        ],
        compiler_params=pltpu.CompilerParams(vmem_limit_bytes=40 * 2**20),
        cost_estimate=pl.CostEstimate(
            flops=5 * rows * units * 8 * width, bytes_accessed=20 * 2**20, transcendentals=0
        ),
        name="experts_in",
    )(core, own, other, gain, gate, up, down)


def expert_own(core, hidden, down, blocks, cap, width):
    rows, units = hidden.shape
    return pl.pallas_call(
        own_kernel,
        grid_spec=pltpu.PrefetchScalarGridSpec(
            num_scalar_prefetch=1,
            grid=(4,),
            in_specs=[
                pl.BlockSpec((rows, units), lambda i, c: (0, 0)),
                pl.BlockSpec((units, width), lambda i, c: (0, 2 * i + c[0])),
            ],
            out_specs=pl.BlockSpec((blocks, 1, cap, width), lambda i, c: (0, i, 0, 0)),
        ),
        out_shape=jax.ShapeDtypeStruct((blocks, 4, cap, width), jnp.bfloat16),
        compiler_params=pltpu.CompilerParams(vmem_limit_bytes=32 * 2**20),
        cost_estimate=pl.CostEstimate(
            flops=rows * units * 8 * width, bytes_accessed=5 * 2**20, transcendentals=0
        ),
        name="experts_own",
    )(core, hidden, down)


def swap(value):
    return lax.ppermute(value, "core", [(0, 1), (1, 0)])


def layer_block(
    residual,
    queries,
    new_keys,
    new_values,
    key_cache,
    value_cache,
    cache_lengths,
    out_weight,
    norm_gain,
    gate_weight,
    up_weight,
    down_weight,
    routes,
    route_gates,
):
    rows, width = residual.shape
    ways = lax.axis_size("y") * lax.axis_size("core")
    share = width // ways
    planes = lax.axis_size("z")
    chips = lax.axis_size("x") * lax.axis_size("y")
    core = lax.axis_index("core")
    column = lax.axis_index("y") * CORES + core

    attended = attend(queries, new_keys, new_values, key_cache, value_cache, cache_lengths)
    partial = jnp.dot(attended, out_weight, preferred_element_type=jnp.float32)
    pieces = partial.astype(jnp.bfloat16).reshape(rows, ways, share).transpose(1, 0, 2)
    pieces = lax.all_to_all(pieces, GROUP, split_axis=0, concat_axis=0, tiled=True)
    start = column * share
    middle = lax.dynamic_slice_in_dim(residual, start, share, 1).astype(jnp.float32)
    middle = middle + jnp.sum(pieces.astype(jnp.float32), axis=0)
    gain = lax.dynamic_slice_in_dim(norm_gain, start, share, 0)
    gained = (middle * gain).astype(jnp.bfloat16)

    flat_routes = routes.reshape(-1)
    one_hot = (flat_routes[:, None] == jnp.arange(EXPERTS)[None, :]).astype(jnp.int32)
    slot_rank = jnp.sum((jnp.cumsum(one_hot, axis=0) - one_hot) * one_hot, axis=1)
    slot_index = flat_routes * CAP + slot_rank
    slot_match = (slot_index[:, None] == jnp.arange(EXPERTS * CAP)[None, :]).reshape(
        rows, 2, EXPERTS * CAP
    )
    chosen = jnp.any(slot_match, axis=1).astype(jnp.bfloat16)
    blend = jnp.sum(slot_match.astype(jnp.float32) * route_gates[:, :, None], axis=1)

    outgoing = jnp.einsum("ts,tc->sc", chosen, gained, preferred_element_type=jnp.float32)
    outgoing = outgoing.astype(jnp.bfloat16).reshape(EXPERTS, 1, CAP, share)
    outgoing = jnp.broadcast_to(outgoing, (EXPERTS, chips, CAP, share))
    own = lax.all_to_all(
        outgoing.reshape(EXPERTS * chips, CAP, share), CHIPS, split_axis=0, concat_axis=0, tiled=True
    )
    other = swap(own)

    core_index = core.astype(jnp.int32).reshape(1)
    shape = (planes * lax.axis_size("x"), lax.axis_size("y"), CAP, share)
    hidden, send = expert_halves(
        core_index,
        own.reshape(shape),
        other.reshape(shape),
        norm_gain.reshape(ways, 1, share),
        gate_weight,
        up_weight,
        down_weight,
    )
    given = swap(send)
    kept = expert_own(core_index, hidden, down_weight, shape[0], CAP, share)
    total = (kept.astype(jnp.float32) + given.astype(jnp.float32)).astype(jnp.bfloat16)
    returned = lax.all_to_all(
        total.reshape(EXPERTS * chips, CAP, share), CHIPS, split_axis=0, concat_axis=0, tiled=True
    )
    merged = jnp.sum(
        returned.reshape(EXPERTS, chips, CAP, share).astype(jnp.float32), axis=1
    ).reshape(EXPERTS * CAP, share)
    return middle + jnp.dot(blend, merged, precision=lax.Precision.HIGHEST)


def solution(mesh):
    fine = Mesh(mesh.devices.reshape(4, 4, 4, 2), ("z", "x", "y", "core"))
    attn, expert = ("z", "x"), ("y", "core")
    every = attn + expert
    in_specs = (
        P(attn, None),
        P(attn, expert),
        P(attn, expert),
        P(attn, expert),
        P(attn, expert, None, None),
        P(attn, expert, None, None),
        P(attn),
        P(expert, None),
        P(),
        P(None, every),
        P(None, every),
        P(every, None),
        P(attn, None),
        P(attn, None),
    )
    return jax.shard_map(
        layer_block, mesh=fine, in_specs=in_specs, out_specs=P(attn, expert), check_vma=False
    )
```

```python
import functools
import math

import jax
import jax.numpy as jnp
from jax import lax
from jax.experimental import pallas as pl
from jax.experimental.pallas import tpu as pltpu
from jax.sharding import Mesh, PartitionSpec as P

EXPERTS = 4
CAP = 24
CORES = 2
EPSILON = 1e-05

CHIPS = ("z", "x", "y")
GROUP = ("y", "core")


PART = 8


def in_hbm(*arrays):
    return tuple(pltpu.with_memory_space_constraint(array, pltpu.HBM) for array in arrays)


def attend_kernel(
    place, lengths, queries, new_keys, new_values, keys, values, out_weight,
    sent_ref, kept_ref,
    length_buf, query_buf, new_key_buf, new_value_buf, key_buf, value_buf, weight_buf, sems,
):
    rows, head_width = new_keys.shape
    heads = queries.shape[1] // head_width
    _, ys, _, width = weight_buf.shape
    span = keys.shape[2]
    parts = rows // PART
    scale = 1.0 / math.sqrt(head_width)

    copies = [
        (lengths, length_buf),
        (queries, query_buf),
        (new_keys, new_key_buf),
        (new_values, new_value_buf),
    ]
    base = len(copies)
    for cache, target in ((keys, key_buf), (values, value_buf)):
        for p in range(parts):
            some = pl.ds(p * PART, PART)
            copies.append((cache.at[some, 0], target.at[some]))
    for half, side in enumerate((1 - place[0], place[0])):
        for step in range(ys):
            block = 2 * lax.rem(place[1] + step, ys) + side
            columns = pl.ds(pl.multiple_of(block * width, width), width)
            copies.append((out_weight.at[:, columns], weight_buf.at[half, step]))
    copies = [
        pltpu.make_async_copy(source, target, sems.at[i]) for i, (source, target) in enumerate(copies)
    ]
    for copy in copies:
        copy.start()
    for copy in copies[:base]:
        copy.wait()
    copies = copies[base:]

    query_heads = query_buf[...].astype(jnp.float32).reshape(rows, heads, head_width)
    new_key = new_key_buf[...].astype(jnp.float32).reshape(rows, 1, head_width)
    new_value = new_value_buf[...].astype(jnp.float32).reshape(rows, 1, head_width)
    fresh = jnp.sum(query_heads * new_key, axis=2, keepdims=True) * scale
    query_heads = query_heads.astype(jnp.bfloat16)
    position = lax.broadcasted_iota(jnp.int32, (heads, span), 1)
    scores = []
    for p in range(parts):
        copies[p].wait()
        some = slice(p * PART, (p + 1) * PART)
        product = jnp.einsum(
            "bhd,bld->bhl", query_heads[some], key_buf[some], preferred_element_type=jnp.float32
        )
        for i in range(PART):
            visible = position < length_buf[0, p * PART + i]
            scores.append(jnp.where(visible, product[i] * scale, -jnp.inf))
    scores = jnp.stack(scores)
    largest = jnp.maximum(jnp.max(scores, axis=2, keepdims=True), fresh)
    exp_scores = jnp.exp(scores - largest)
    exp_fresh = jnp.exp(fresh - largest)
    inverse = 1.0 / (jnp.sum(exp_scores, axis=2, keepdims=True) + exp_fresh)
    weights = (exp_scores * inverse).astype(jnp.bfloat16)
    weights_new = (exp_fresh * inverse).astype(jnp.bfloat16).astype(jnp.float32)
    attended = []
    for p in range(parts):
        copies[parts + p].wait()
        some = slice(p * PART, (p + 1) * PART)
        mixture = jnp.einsum(
            "bhl,bld->bhd", weights[some], value_buf[some], preferred_element_type=jnp.float32
        )
        attended.append(mixture + weights_new[some] * new_value[some])
    attended = jnp.concatenate(attended, axis=0).reshape(rows, heads * head_width)
    attended = attended.astype(jnp.bfloat16)
    for half, target in enumerate((sent_ref, kept_ref)):
        for y in range(ys):
            copies[2 * parts + half * ys + y].wait()
            out = jnp.dot(attended, weight_buf[half, y], preferred_element_type=jnp.float32)
            target[y] = out.astype(target.dtype)


def attend(place, lengths, queries, new_keys, new_values, keys, values, out_weight):
    rows, span, head_width = keys.shape[0], keys.shape[2], keys.shape[3]
    ys, width = 4, queries.shape[1]
    scalars = pl.BlockSpec(memory_space=pltpu.SMEM)
    inside = pl.BlockSpec(memory_space=pltpu.VMEM)
    outside = pl.BlockSpec(memory_space=pltpu.HBM)
    return pl.pallas_call(
        attend_kernel,
        in_specs=[scalars] + [outside] * 7,
        out_specs=[inside] * 2,
        out_shape=[
            jax.ShapeDtypeStruct((ys, rows, width), jnp.bfloat16),
            jax.ShapeDtypeStruct((ys, rows, width), jnp.float32),
        ],
        scratch_shapes=[
            pltpu.SMEM((1, rows), jnp.int32),
            pltpu.VMEM((rows, width), jnp.bfloat16),
            pltpu.VMEM((rows, head_width), jnp.bfloat16),
            pltpu.VMEM((rows, head_width), jnp.bfloat16),
            pltpu.VMEM((rows, span, head_width), jnp.bfloat16),
            pltpu.VMEM((rows, span, head_width), jnp.bfloat16),
            pltpu.VMEM((2, ys, width, width), jnp.bfloat16),
            pltpu.SemaphoreType.DMA((4 + 2 * rows // PART + 2 * ys,)),
        ],
        compiler_params=pltpu.CompilerParams(vmem_limit_bytes=32 * 2**20),
        cost_estimate=pl.CostEstimate(
            flops=rows * width * width * 8, bytes_accessed=15 * 2**20, transcendentals=0
        ),
        name="attend",
    )(place, *in_hbm(lengths, queries, new_keys, new_values, keys, values, out_weight))


def gate_up_copies(side, gate, up, target, sems):
    ys, width, units = target.shape[0], target.shape[1], gate.shape[1]
    copies = []
    for y in range(ys):
        rows = pl.ds(pl.multiple_of((2 * y + side) * width, width), width)
        copies.append((gate.at[rows, :], target.at[y, :, pl.ds(0, units)]))
        copies.append((up.at[rows, :], target.at[y, :, pl.ds(units, units)]))
    return [pltpu.make_async_copy(s, t, sems.at[i]) for i, (s, t) in enumerate(copies)]


def load_kernel(core, gate, up, own_weight, other_weight, sems):
    copies = gate_up_copies(core[0], gate, up, own_weight, sems.at[0])
    copies += gate_up_copies(1 - core[0], gate, up, other_weight, sems.at[1])
    for copy in copies:
        copy.start()
    for copy in copies:
        copy.wait()


def load_weights(core, gate, up):
    ys, width, units = 4, 768, gate.shape[1]
    inside = pl.BlockSpec(memory_space=pltpu.VMEM)
    outside = pl.BlockSpec(memory_space=pltpu.HBM)
    return pl.pallas_call(
        load_kernel,
        in_specs=[pl.BlockSpec(memory_space=pltpu.SMEM)] + [outside] * 2,
        out_specs=[inside] * 2,
        out_shape=[jax.ShapeDtypeStruct((ys, width, 2 * units), jnp.bfloat16)] * 2,
        scratch_shapes=[pltpu.SemaphoreType.DMA((2, 2 * ys))],
        compiler_params=pltpu.CompilerParams(vmem_limit_bytes=16 * 2**20),
        cost_estimate=pl.CostEstimate(flops=0, bytes_accessed=19 * 2**20, transcendentals=0),
        name="load_weights",
    )(core, *in_hbm(gate, up))


def down_copies(side, down, down_other, target, sems):
    ys, width, units = target.shape[0], target.shape[2], down.shape[0]
    copies = []
    for y in range(ys):
        columns = pl.ds(pl.multiple_of((2 * y + side) * width, width), width)
        copies.append((down.at[:, columns], target.at[y, pl.ds(0, units), :]))
        copies.append((down_other.at[:, columns], target.at[y, pl.ds(units, units), :]))
    return [pltpu.make_async_copy(s, t, sems.at[i]) for i, (s, t) in enumerate(copies)]


def add_products(side, source, gain, weight, total, squares):
    blocks, ys, cap, width = source.shape
    rows = blocks * cap
    for y in range(ys):
        wide = source[:, y].astype(jnp.float32).reshape(rows, width)
        inverse = 1.0 / gain[pl.ds(2 * y + side, 1), :]
        parts = wide * wide * (inverse * inverse)
        step = parts[:, 0:128]
        for j in range(1, width // 128):
            step = step + parts[:, j * 128 : (j + 1) * 128]
        product = jnp.dot(wide.astype(jnp.bfloat16), weight[y], preferred_element_type=jnp.float32)
        if total is None:
            total, squares = product, step
        else:
            total, squares = total + product, squares + step
    return total, squares


def first_kernel(
    core, own, gain, weight, down, down_other, total_ref, squares_ref, out_weight, sems
):
    copies = down_copies(core[0], down, down_other, out_weight, sems)
    for copy in copies:
        copy.start()
    total, squares = add_products(core[0], own, gain, weight, None, None)
    total_ref[...] = total
    squares_ref[...] = squares
    for copy in copies:
        copy.wait()


def second_kernel(core, other, gain, weight, total_ref, squares_ref, hidden_ref):
    ys, width = other.shape[1], other.shape[3]
    total, squares = add_products(
        1 - core[0], other, gain, weight, total_ref[...], squares_ref[...]
    )
    mean = jnp.sum(squares, axis=1, keepdims=True) * (1.0 / (CORES * ys * width))
    total = total * lax.rsqrt(mean + EPSILON)
    units = total.shape[1] // 2
    gate_sum, up_sum = total[:, :units], total[:, units:]
    hidden_ref[...] = (gate_sum / (1.0 + jnp.exp(-gate_sum)) * up_sum).astype(jnp.bfloat16)


def out_kernel(hidden, hidden_other, weight, out_ref):
    blocks, _, cap, width = out_ref.shape
    units = hidden.shape[1]
    out = jnp.dot(hidden[...], weight[0, :units], preferred_element_type=jnp.float32)
    out += jnp.dot(hidden_other[...], weight[0, units:], preferred_element_type=jnp.float32)
    out_ref[...] = out.reshape(blocks, 1, cap, width).astype(out_ref.dtype)


def experts_first(core, own, gain, weight, down, down_other):
    blocks, ys, cap, width = own.shape
    rows, units = blocks * cap, down.shape[0]
    inside = pl.BlockSpec(memory_space=pltpu.VMEM)
    outside = pl.BlockSpec(memory_space=pltpu.HBM)
    return pl.pallas_call(
        first_kernel,
        in_specs=[pl.BlockSpec(memory_space=pltpu.SMEM)] + [inside] * 3 + [outside, pl.BlockSpec(memory_space=pl.ANY)],
        out_specs=[inside] * 3,
        out_shape=[
            jax.ShapeDtypeStruct((rows, 2 * units), jnp.float32),
            jax.ShapeDtypeStruct((rows, 128), jnp.float32),
            jax.ShapeDtypeStruct((ys, 2 * units, width), jnp.bfloat16),
        ],
        scratch_shapes=[pltpu.SemaphoreType.DMA((2 * ys,))],
        compiler_params=pltpu.CompilerParams(vmem_limit_bytes=16 * 2**20),
        cost_estimate=pl.CostEstimate(
            flops=4 * rows * units * ys * width, bytes_accessed=12 * 2**20, transcendentals=0
        ),
        name="experts_first",
    )(core, own, gain, weight, *in_hbm(down), down_other)


def experts_second(core, other, gain, weight, total, squares):
    rows, units = total.shape[0], total.shape[1] // 2
    ys, width = weight.shape[0], weight.shape[1]
    inside = pl.BlockSpec(memory_space=pltpu.VMEM)
    return pl.pallas_call(
        second_kernel,
        in_specs=[pl.BlockSpec(memory_space=pltpu.SMEM)] + [inside] * 5,
        out_specs=inside,
        out_shape=jax.ShapeDtypeStruct((rows, units), jnp.bfloat16),
        compiler_params=pltpu.CompilerParams(vmem_limit_bytes=16 * 2**20),
        cost_estimate=pl.CostEstimate(
            flops=4 * rows * units * ys * width, bytes_accessed=12 * 2**20, transcendentals=0
        ),
        name="experts_second",
    )(core, pltpu.with_memory_space_constraint(other, pltpu.VMEM), gain, weight, total, squares)


def experts_out(hidden, hidden_other, weight, blocks):
    rows, units = hidden.shape
    ys, _, width = weight.shape
    cap = rows // blocks
    return pl.pallas_call(
        out_kernel,
        grid=(ys,),
        in_specs=[
            pl.BlockSpec((rows, units), lambda i: (0, 0)),
            pl.BlockSpec((rows, units), lambda i: (0, 0)),
            pl.BlockSpec((1, 2 * units, width), lambda i: (i, 0, 0)),
        ],
        out_specs=pl.BlockSpec((blocks, 1, cap, width), lambda i: (0, i, 0, 0)),
        out_shape=jax.ShapeDtypeStruct((blocks, ys, cap, width), jnp.bfloat16),
        compiler_params=pltpu.CompilerParams(vmem_limit_bytes=20 * 2**20),
        cost_estimate=pl.CostEstimate(
            flops=4 * rows * units * ys * width, bytes_accessed=8 * 2**20, transcendentals=0
        ),
        name="experts_out",
    )(hidden, hidden_other, weight)


def swap(value):
    return lax.ppermute(value, "core", [(0, 1), (1, 0)])


def layer_block(
    residual,
    queries,
    new_keys,
    new_values,
    key_cache,
    value_cache,
    cache_lengths,
    out_weight,
    norm_gain,
    gate_weight,
    up_weight,
    down_weight,
    routes,
    route_gates,
):
    rows, width = residual.shape
    ways = lax.axis_size("y") * lax.axis_size("core")
    share = width // ways
    planes = lax.axis_size("z")
    chips = lax.axis_size("x") * lax.axis_size("y")
    core = lax.axis_index("core")
    column = lax.axis_index("y") * CORES + core

    core_index = core.astype(jnp.int32).reshape(1)
    place = jnp.stack([core, lax.axis_index("y")]).astype(jnp.int32)
    sent, kept = attend(
        place, cache_lengths.reshape(1, -1), queries, new_keys, new_values, key_cache, value_cache, out_weight
    )
    first = kept + swap(sent).astype(jnp.float32)
    chips_y = lax.axis_size("y")
    pieces = [
        lax.ppermute(
            first[s].astype(jnp.bfloat16), "y", [(i, (i + s) % chips_y) for i in range(chips_y)]
        )
        for s in range(1, chips_y)
    ]
    gains = norm_gain.reshape(ways, share)
    first, gains, gate_weight, up_weight, down_weight = lax.optimization_barrier(
        (first, gains, gate_weight, up_weight, down_weight)
    )
    down_other = swap(down_weight)
    own_weight, other_weight = load_weights(core_index, gate_weight, up_weight)
    pieces, own_weight, other_weight = lax.optimization_barrier((pieces, own_weight, other_weight))
    start = column * share
    middle = lax.dynamic_slice_in_dim(residual, start, share, 1).astype(jnp.float32)
    middle = middle + first[0] + sum(piece.astype(jnp.float32) for piece in pieces)
    gain = lax.dynamic_slice_in_dim(norm_gain, start, share, 0)
    gained = (middle * gain).astype(jnp.bfloat16)

    named = routes[:, :, None] == jnp.arange(EXPERTS)[None, None, :]
    coef = jnp.sum(jnp.where(named, route_gates[:, :, None], 0.0), axis=1)
    taken = jnp.any(named, axis=1)
    before = jnp.arange(rows)[:, None] > jnp.arange(rows)[None, :]
    rank = jnp.dot(
        before.astype(jnp.bfloat16), taken.astype(jnp.bfloat16), preferred_element_type=jnp.float32
    )
    match = taken[:, :, None] & (rank.astype(jnp.int32)[:, :, None] == jnp.arange(CAP)[None, None, :])
    chosen = match.astype(jnp.bfloat16).reshape(rows, EXPERTS * CAP)
    blend = jnp.where(match, coef[:, :, None], 0.0).reshape(rows, EXPERTS * CAP)

    outgoing = jnp.einsum("ts,tc->sc", chosen, gained, preferred_element_type=jnp.float32)
    outgoing = outgoing.astype(jnp.bfloat16).reshape(EXPERTS, 1, CAP, share)
    outgoing = jnp.broadcast_to(outgoing, (EXPERTS, chips, CAP, share))
    own = lax.all_to_all(
        outgoing.reshape(EXPERTS * chips, CAP, share), CHIPS, split_axis=0, concat_axis=0, tiled=True
    )
    other = swap(own)

    shape = (planes * lax.axis_size("x"), lax.axis_size("y"), CAP, share)
    total, squares, out_weights = experts_first(
        core_index, own.reshape(shape), gains, own_weight, down_weight, down_other
    )
    hidden = experts_second(core_index, other.reshape(shape), gains, other_weight, total, squares)
    outs = experts_out(hidden, swap(hidden), out_weights, shape[0])
    returned = lax.all_to_all(
        outs.reshape(EXPERTS * chips, CAP, share), CHIPS, split_axis=0, concat_axis=0, tiled=True
    )
    merged = jnp.sum(
        returned.reshape(EXPERTS, chips, CAP, share).astype(jnp.float32), axis=1
    ).reshape(EXPERTS * CAP, share)
    return middle + jnp.dot(blend, merged, precision=lax.Precision.HIGHEST)


def solution(mesh):
    fine = Mesh(mesh.devices.reshape(4, 4, 4, 2), ("z", "x", "y", "core"))
    attn, expert = ("z", "x"), ("y", "core")
    every = attn + expert
    in_specs = (
        P(attn, None),
        P(attn, expert),
        P(attn, expert),
        P(attn, expert),
        P(attn, expert, None, None),
        P(attn, expert, None, None),
        P(attn),
        P(expert, None),
        P(),
        P(None, every),
        P(None, every),
        P(every, None),
        P(attn, None),
        P(attn, None),
    )
    return jax.shard_map(
        layer_block, mesh=fine, in_specs=in_specs, out_specs=P(attn, expert), check_vma=False
    )
```

```python
import functools
import math

import jax
import jax.numpy as jnp
from jax import lax
from jax.experimental import pallas as pl
from jax.experimental.pallas import tpu as pltpu
from jax.sharding import Mesh, PartitionSpec as P

EXPERTS = 4
CAP = 24
CORES = 2
EPSILON = 1e-05

EVERY = ("z", "x", "y", "core")
FLIP = 2
CHIP_ORDERS = [
    [
        (((z ^ (FLIP * c)) * 4 + (x ^ (FLIP * c))) * 4 + (y ^ (FLIP * c))) * CORES + c
        for y in range(4)
        for z in range(4)
        for x in range(4)
    ]
    for c in range(CORES)
]


def exchange(blocks):
    flat = blocks.reshape(64, *blocks.shape[3:])
    flat = lax.all_to_all(
        flat, EVERY, split_axis=0, concat_axis=0, axis_index_groups=CHIP_ORDERS, tiled=True
    )
    return flat.reshape(blocks.shape)


PART = 8


def in_hbm(*arrays):
    return tuple(pltpu.with_memory_space_constraint(array, pltpu.HBM) for array in arrays)


def attend_kernel(
    place, lengths, queries, new_keys, new_values, keys, values, out_weight,
    sent_ref, kept_ref,
    length_buf, query_buf, new_key_buf, new_value_buf, key_buf, value_buf, weight_buf, sems,
):
    rows, head_width = new_keys.shape
    heads = queries.shape[1] // head_width
    _, ys, _, width = weight_buf.shape
    span = keys.shape[2]
    parts = rows // PART
    scale = 1.0 / math.sqrt(head_width)

    copies = [
        (lengths, length_buf),
        (queries, query_buf),
        (new_keys, new_key_buf),
        (new_values, new_value_buf),
    ]
    base = len(copies)
    for cache, target in ((keys, key_buf), (values, value_buf)):
        for p in range(parts):
            some = pl.ds(p * PART, PART)
            copies.append((cache.at[some, 0], target.at[some]))
    for half, side in enumerate((1 - place[0], place[0])):
        for step in range(ys):
            block = 2 * lax.rem(place[1] + step, ys) + side
            columns = pl.ds(pl.multiple_of(block * width, width), width)
            copies.append((out_weight.at[:, columns], weight_buf.at[half, step]))
    copies = [
        pltpu.make_async_copy(source, target, sems.at[i]) for i, (source, target) in enumerate(copies)
    ]
    for copy in copies:
        copy.start()
    for copy in copies[:base]:
        copy.wait()
    copies = copies[base:]

    query_heads = query_buf[...].astype(jnp.float32).reshape(rows, heads, head_width)
    new_key = new_key_buf[...].astype(jnp.float32).reshape(rows, 1, head_width)
    new_value = new_value_buf[...].astype(jnp.float32).reshape(rows, 1, head_width)
    fresh = jnp.sum(query_heads * new_key, axis=2, keepdims=True) * scale
    query_heads = query_heads.astype(jnp.bfloat16)
    position = lax.broadcasted_iota(jnp.int32, (heads, span), 1)
    scores = []
    for p in range(parts):
        copies[p].wait()
        some = slice(p * PART, (p + 1) * PART)
        product = jnp.einsum(
            "bhd,bld->bhl", query_heads[some], key_buf[some], preferred_element_type=jnp.float32
        )
        for i in range(PART):
            visible = position < length_buf[0, p * PART + i]
            scores.append(jnp.where(visible, product[i] * scale, -jnp.inf))
    scores = jnp.stack(scores)
    largest = jnp.maximum(jnp.max(scores, axis=2, keepdims=True), fresh)
    exp_scores = jnp.exp(scores - largest)
    exp_fresh = jnp.exp(fresh - largest)
    inverse = 1.0 / (jnp.sum(exp_scores, axis=2, keepdims=True) + exp_fresh)
    weights = (exp_scores * inverse).astype(jnp.bfloat16)
    weights_new = (exp_fresh * inverse).astype(jnp.bfloat16).astype(jnp.float32)
    attended = []
    for p in range(parts):
        copies[parts + p].wait()
        some = slice(p * PART, (p + 1) * PART)
        mixture = jnp.einsum(
            "bhl,bld->bhd", weights[some], value_buf[some], preferred_element_type=jnp.float32
        )
        attended.append(mixture + weights_new[some] * new_value[some])
    attended = jnp.concatenate(attended, axis=0).reshape(rows, heads * head_width)
    attended = attended.astype(jnp.bfloat16)
    for half, target in enumerate((sent_ref, kept_ref)):
        for y in range(ys):
            copies[2 * parts + half * ys + y].wait()
            out = jnp.dot(attended, weight_buf[half, y], preferred_element_type=jnp.float32)
            target[y] = out.astype(target.dtype)


def attend(place, lengths, queries, new_keys, new_values, keys, values, out_weight):
    rows, span, head_width = keys.shape[0], keys.shape[2], keys.shape[3]
    ys, width = 4, queries.shape[1]
    scalars = pl.BlockSpec(memory_space=pltpu.SMEM)
    inside = pl.BlockSpec(memory_space=pltpu.VMEM)
    outside = pl.BlockSpec(memory_space=pltpu.HBM)
    return pl.pallas_call(
        attend_kernel,
        in_specs=[scalars] + [outside] * 7,
        out_specs=[inside] * 2,
        out_shape=[
            jax.ShapeDtypeStruct((ys, rows, width), jnp.bfloat16),
            jax.ShapeDtypeStruct((ys, rows, width), jnp.float32),
        ],
        scratch_shapes=[
            pltpu.SMEM((1, rows), jnp.int32),
            pltpu.VMEM((rows, width), jnp.bfloat16),
            pltpu.VMEM((rows, head_width), jnp.bfloat16),
            pltpu.VMEM((rows, head_width), jnp.bfloat16),
            pltpu.VMEM((rows, span, head_width), jnp.bfloat16),
            pltpu.VMEM((rows, span, head_width), jnp.bfloat16),
            pltpu.VMEM((2, ys, width, width), jnp.bfloat16),
            pltpu.SemaphoreType.DMA((4 + 2 * rows // PART + 2 * ys,)),
        ],
        compiler_params=pltpu.CompilerParams(vmem_limit_bytes=32 * 2**20),
        cost_estimate=pl.CostEstimate(
            flops=rows * width * width * 8, bytes_accessed=15 * 2**20, transcendentals=0
        ),
        name="attend",
    )(place, *in_hbm(lengths, queries, new_keys, new_values, keys, values, out_weight))


def gate_up_copies(side, gate, up, target, sems):
    ys, width, units = target.shape[0], target.shape[1], gate.shape[1]
    copies = []
    for y in range(ys):
        rows = pl.ds(pl.multiple_of((2 * y + side) * width, width), width)
        copies.append((gate.at[rows, :], target.at[y, :, pl.ds(0, units)]))
        copies.append((up.at[rows, :], target.at[y, :, pl.ds(units, units)]))
    return [pltpu.make_async_copy(s, t, sems.at[i]) for i, (s, t) in enumerate(copies)]


def load_kernel(core, gate, up, own_weight, sems):
    copies = gate_up_copies(core[0], gate, up, own_weight, sems)
    for copy in copies:
        copy.start()
    for copy in copies:
        copy.wait()


def load_weights(core, gate, up):
    ys, width, units = 4, 768, gate.shape[1]
    inside = pl.BlockSpec(memory_space=pltpu.VMEM)
    outside = pl.BlockSpec(memory_space=pltpu.HBM)
    return pl.pallas_call(
        load_kernel,
        in_specs=[pl.BlockSpec(memory_space=pltpu.SMEM)] + [outside] * 2,
        out_specs=inside,
        out_shape=jax.ShapeDtypeStruct((ys, width, 2 * units), jnp.bfloat16),
        scratch_shapes=[pltpu.SemaphoreType.DMA((2 * ys,))],
        compiler_params=pltpu.CompilerParams(vmem_limit_bytes=16 * 2**20),
        cost_estimate=pl.CostEstimate(flops=0, bytes_accessed=9 * 2**20, transcendentals=0),
        name="load_weights",
    )(core, *in_hbm(gate, up))


def down_copies(side, down, down_other, target, sems):
    ys, width, units = target.shape[0], target.shape[2], down.shape[0]
    copies = []
    for y in range(ys):
        columns = pl.ds(pl.multiple_of((2 * y + side) * width, width), width)
        copies.append((down.at[:, columns], target.at[y, pl.ds(0, units), :]))
        copies.append((down_other.at[:, columns], target.at[y, pl.ds(units, units), :]))
    return [pltpu.make_async_copy(s, t, sems.at[i]) for i, (s, t) in enumerate(copies)]


def add_products(side, source, gain, weight, total, squares):
    ys, zs, xs, cap, width = source.shape
    rows = zs * xs * cap
    flip = FLIP * side
    for y in range(ys):
        parts = [
            source[y ^ flip, z ^ flip, pl.ds(x ^ flip, FLIP)]
            for z in range(zs)
            for x in range(0, xs, FLIP)
        ]
        wide = jnp.concatenate(parts, axis=0).astype(jnp.float32).reshape(rows, width)
        inverse = 1.0 / gain[pl.ds(2 * y + side, 1), :]
        parts = wide * wide * (inverse * inverse)
        step = parts[:, 0:128]
        for j in range(1, width // 128):
            step = step + parts[:, j * 128 : (j + 1) * 128]
        product = jnp.dot(wide.astype(jnp.bfloat16), weight[y], preferred_element_type=jnp.float32)
        if total is None:
            total, squares = product, step
        else:
            total, squares = total + product, squares + step
    return total, squares


def first_kernel(
    core, own, gain, weight, gate, up, down, down_other,
    total_ref, squares_ref, other_weight, out_weight, sems,
):
    copies = gate_up_copies(1 - core[0], gate, up, other_weight, sems.at[0])
    copies += down_copies(core[0], down, down_other, out_weight, sems.at[1])
    for copy in copies:
        copy.start()
    total, squares = add_products(core[0], own, gain, weight, None, None)
    total_ref[...] = total
    squares_ref[...] = squares
    for copy in copies:
        copy.wait()


def second_kernel(core, other, gain, weight, total_ref, squares_ref, hidden_ref):
    ys, width = other.shape[0], other.shape[4]
    total, squares = add_products(
        1 - core[0], other, gain, weight, total_ref[...], squares_ref[...]
    )
    mean = jnp.sum(squares, axis=1, keepdims=True) * (1.0 / (CORES * ys * width))
    total = total * lax.rsqrt(mean + EPSILON)
    units = total.shape[1] // 2
    gate_sum, up_sum = total[:, :units], total[:, units:]
    hidden_ref[...] = (gate_sum / (1.0 + jnp.exp(-gate_sum)) * up_sum).astype(jnp.bfloat16)


def out_kernel(core, hidden, hidden_other, weight, out_ref, buf, sems):
    ys, zs, xs, cap, width = out_ref.shape
    flip = FLIP * core[0]
    both = jnp.concatenate([hidden[...], hidden_other[...]], axis=1)
    copies = []
    for y in range(ys):
        out = jnp.dot(both, weight[y], preferred_element_type=jnp.float32)
        buf[y] = out.reshape(zs, xs, cap, width).astype(buf.dtype)
        for z in range(zs):
            for x in range(0, xs, FLIP):
                copies.append(
                    pltpu.make_async_copy(
                        buf.at[y, z, pl.ds(x, FLIP)],
                        out_ref.at[y ^ flip, z ^ flip, pl.ds(x ^ flip, FLIP)],
                        sems.at[len(copies)],
                    )
                )
                copies[-1].start()
    for copy in copies:
        copy.wait()


def experts_first(core, own, gain, weight, gate, up, down, down_other):
    ys, zs, xs, cap, width = own.shape
    rows, units = zs * xs * cap, down.shape[0]
    inside = pl.BlockSpec(memory_space=pltpu.VMEM)
    outside = pl.BlockSpec(memory_space=pltpu.HBM)
    return pl.pallas_call(
        first_kernel,
        in_specs=[pl.BlockSpec(memory_space=pltpu.SMEM)] + [inside] * 3 + [outside] * 3 + [pl.BlockSpec(memory_space=pl.ANY)],
        out_specs=[inside] * 4,
        out_shape=[
            jax.ShapeDtypeStruct((rows, 2 * units), jnp.float32),
            jax.ShapeDtypeStruct((rows, 128), jnp.float32),
            jax.ShapeDtypeStruct((ys, width, 2 * units), jnp.bfloat16),
            jax.ShapeDtypeStruct((ys, 2 * units, width), jnp.bfloat16),
        ],
        scratch_shapes=[pltpu.SemaphoreType.DMA((2, 2 * ys))],
        compiler_params=pltpu.CompilerParams(vmem_limit_bytes=16 * 2**20),
        cost_estimate=pl.CostEstimate(
            flops=4 * rows * units * ys * width, bytes_accessed=12 * 2**20, transcendentals=0
        ),
        name="experts_first",
    )(core, own, gain, weight, *in_hbm(gate, up, down), down_other)


def experts_second(core, other, gain, weight, total, squares):
    rows, units = total.shape[0], total.shape[1] // 2
    ys, width = weight.shape[0], weight.shape[1]
    inside = pl.BlockSpec(memory_space=pltpu.VMEM)
    return pl.pallas_call(
        second_kernel,
        in_specs=[pl.BlockSpec(memory_space=pltpu.SMEM)] + [inside] * 5,
        out_specs=inside,
        out_shape=jax.ShapeDtypeStruct((rows, units), jnp.bfloat16),
        compiler_params=pltpu.CompilerParams(vmem_limit_bytes=16 * 2**20),
        cost_estimate=pl.CostEstimate(
            flops=4 * rows * units * ys * width, bytes_accessed=12 * 2**20, transcendentals=0
        ),
        name="experts_second",
    )(core, pltpu.with_memory_space_constraint(other, pltpu.VMEM), gain, weight, total, squares)


def experts_out(core, hidden, hidden_other, weight, shape):
    rows, units = hidden.shape
    ys, zs, xs, cap, width = shape
    inside = pl.BlockSpec(memory_space=pltpu.VMEM)
    return pl.pallas_call(
        out_kernel,
        in_specs=[pl.BlockSpec(memory_space=pltpu.SMEM)] + [inside] * 3,
        out_specs=pl.BlockSpec(memory_space=pltpu.HBM),
        out_shape=jax.ShapeDtypeStruct(shape, jnp.bfloat16),
        scratch_shapes=[
            pltpu.VMEM((ys, zs, xs, cap, width), jnp.bfloat16),
            pltpu.SemaphoreType.DMA((ys * zs * xs // FLIP,)),
        ],
        compiler_params=pltpu.CompilerParams(vmem_limit_bytes=20 * 2**20),
        cost_estimate=pl.CostEstimate(
            flops=4 * rows * units * ys * width, bytes_accessed=8 * 2**20, transcendentals=0
        ),
        name="experts_out",
    )(core, hidden, hidden_other, weight)


def swap(value):
    return lax.ppermute(value, "core", [(0, 1), (1, 0)])


def layer_block(
    residual,
    queries,
    new_keys,
    new_values,
    key_cache,
    value_cache,
    cache_lengths,
    out_weight,
    norm_gain,
    gate_weight,
    up_weight,
    down_weight,
    routes,
    route_gates,
):
    rows, width = residual.shape
    ways = lax.axis_size("y") * lax.axis_size("core")
    share = width // ways
    shape = (lax.axis_size("y"), lax.axis_size("z"), lax.axis_size("x"), CAP, share)
    core = lax.axis_index("core")
    column = lax.axis_index("y") * CORES + core

    core_index = core.astype(jnp.int32).reshape(1)
    place = jnp.stack([core, lax.axis_index("y")]).astype(jnp.int32)
    sent, kept = attend(
        place, cache_lengths.reshape(1, -1), queries, new_keys, new_values, key_cache, value_cache, out_weight
    )
    first = kept + swap(sent).astype(jnp.float32)
    chips_y = lax.axis_size("y")
    pieces = [
        lax.ppermute(
            first[s].astype(jnp.bfloat16), "y", [(i, (i + s) % chips_y) for i in range(chips_y)]
        )
        for s in range(1, chips_y)
    ]
    gains = norm_gain.reshape(ways, share)
    first, gains, gate_weight, up_weight, down_weight = lax.optimization_barrier(
        (first, gains, gate_weight, up_weight, down_weight)
    )
    down_other = swap(down_weight)
    own_weight = load_weights(core_index, gate_weight, up_weight)
    pieces, own_weight = lax.optimization_barrier((pieces, own_weight))
    start = column * share
    middle = lax.dynamic_slice_in_dim(residual, start, share, 1).astype(jnp.float32)
    middle = middle + first[0] + sum(piece.astype(jnp.float32) for piece in pieces)
    gain = lax.dynamic_slice_in_dim(norm_gain, start, share, 0)
    gained = (middle * gain).astype(jnp.bfloat16)

    order = jnp.arange(EXPERTS) ^ (FLIP * core)
    named = routes[:, :, None] == order[None, None, :]
    coef = jnp.sum(jnp.where(named, route_gates[:, :, None], 0.0), axis=1)
    taken = jnp.any(named, axis=1)
    before = jnp.arange(rows)[:, None] > jnp.arange(rows)[None, :]
    rank = jnp.dot(
        before.astype(jnp.bfloat16), taken.astype(jnp.bfloat16), preferred_element_type=jnp.float32
    )
    match = taken[:, :, None] & (rank.astype(jnp.int32)[:, :, None] == jnp.arange(CAP)[None, None, :])
    chosen = match.astype(jnp.bfloat16).reshape(rows, EXPERTS * CAP)
    blend = jnp.where(match, coef[:, :, None], 0.0).reshape(rows, EXPERTS * CAP)

    outgoing = jnp.einsum("ts,tc->sc", chosen, gained, preferred_element_type=jnp.float32)
    outgoing = outgoing.astype(jnp.bfloat16).reshape(1, EXPERTS, 1, CAP, share)
    own = exchange(jnp.broadcast_to(outgoing, shape))
    other = swap(own)

    total, squares, other_weight, out_weights = experts_first(
        core_index, own, gains, own_weight, gate_weight, up_weight, down_weight, down_other
    )
    hidden = experts_second(core_index, other, gains, other_weight, total, squares)
    outs = experts_out(core_index, hidden, swap(hidden), out_weights, shape)
    returned = exchange(outs)
    merged = jnp.sum(returned.astype(jnp.float32), axis=(0, 2)).reshape(EXPERTS * CAP, share)
    return middle + jnp.dot(blend, merged, precision=lax.Precision.HIGHEST)


def solution(mesh):
    fine = Mesh(mesh.devices.reshape(4, 4, 4, 2), ("z", "x", "y", "core"))
    attn, expert = ("z", "x"), ("y", "core")
    every = attn + expert
    in_specs = (
        P(attn, None),
        P(attn, expert),
        P(attn, expert),
        P(attn, expert),
        P(attn, expert, None, None),
        P(attn, expert, None, None),
        P(attn),
        P(expert, None),
        P(),
        P(None, every),
        P(None, every),
        P(every, None),
        P(attn, None),
        P(attn, None),
    )
    return jax.shard_map(
        layer_block, mesh=fine, in_specs=in_specs, out_specs=P(attn, expert), check_vma=False
    )
```

```python
import functools
import math

import jax
import jax.numpy as jnp
from jax import lax
from jax.experimental import pallas as pl
from jax.experimental.pallas import tpu as pltpu
from jax.sharding import Mesh, PartitionSpec as P

EXPERTS = 4
CAP = 24
CORES = 2
EPSILON = 1e-05

EVERY = ("z", "x", "y", "core")
FLIP = 2
CHIP_ORDERS = [
    [
        (((z ^ (FLIP * c)) * 4 + (x ^ (FLIP * c))) * 4 + (y ^ (FLIP * c))) * CORES + c
        for y in range(4)
        for z in range(4)
        for x in range(4)
    ]
    for c in range(CORES)
]


def exchange(blocks):
    flat = blocks.reshape(64, *blocks.shape[3:])
    flat = lax.all_to_all(
        flat, EVERY, split_axis=0, concat_axis=0, axis_index_groups=CHIP_ORDERS, tiled=True
    )
    return flat.reshape(blocks.shape)


PART = 8


def in_hbm(*arrays):
    return tuple(pltpu.with_memory_space_constraint(array, pltpu.HBM) for array in arrays)


def attend_kernel(
    place, lengths, queries, new_keys, new_values, keys, values, out_weight,
    sent_ref, attended_ref, own_weight,
    length_buf, query_buf, new_key_buf, new_value_buf, key_buf, value_buf, weight_buf, sems,
):
    rows, head_width = new_keys.shape
    heads = queries.shape[1] // head_width
    ys, _, width = weight_buf.shape
    span = keys.shape[2]
    parts = rows // PART
    scale = 1.0 / math.sqrt(head_width)

    copies = [
        (lengths, length_buf),
        (queries, query_buf),
        (new_keys, new_key_buf),
        (new_values, new_value_buf),
    ]
    base = len(copies)
    for cache, target in ((keys, key_buf), (values, value_buf)):
        for p in range(parts):
            some = pl.ds(p * PART, PART)
            copies.append((cache.at[some, 0], target.at[some]))
    for side, target in ((1 - place[0], weight_buf), (place[0], own_weight)):
        for step in range(ys):
            block = 2 * lax.rem(place[1] + step, ys) + side
            columns = pl.ds(pl.multiple_of(block * width, width), width)
            copies.append((out_weight.at[:, columns], target.at[step]))
    copies = [
        pltpu.make_async_copy(source, target, sems.at[i]) for i, (source, target) in enumerate(copies)
    ]
    for copy in copies:
        copy.start()
    for copy in copies[:base]:
        copy.wait()
    copies = copies[base:]

    query_heads = query_buf[...].astype(jnp.float32).reshape(rows, heads, head_width)
    new_key = new_key_buf[...].astype(jnp.float32).reshape(rows, 1, head_width)
    new_value = new_value_buf[...].astype(jnp.float32).reshape(rows, 1, head_width)
    fresh = jnp.sum(query_heads * new_key, axis=2, keepdims=True) * scale
    query_heads = query_heads.astype(jnp.bfloat16)
    position = lax.broadcasted_iota(jnp.int32, (heads, span), 1)
    scores = []
    for p in range(parts):
        copies[p].wait()
        some = slice(p * PART, (p + 1) * PART)
        product = jnp.einsum(
            "bhd,bld->bhl", query_heads[some], key_buf[some], preferred_element_type=jnp.float32
        )
        for i in range(PART):
            visible = position < length_buf[0, p * PART + i]
            scores.append(jnp.where(visible, product[i] * scale, -jnp.inf))
    scores = jnp.stack(scores)
    largest = jnp.maximum(jnp.max(scores, axis=2, keepdims=True), fresh)
    exp_scores = jnp.exp(scores - largest)
    exp_fresh = jnp.exp(fresh - largest)
    inverse = 1.0 / (jnp.sum(exp_scores, axis=2, keepdims=True) + exp_fresh)
    weights = (exp_scores * inverse).astype(jnp.bfloat16)
    weights_new = (exp_fresh * inverse).astype(jnp.bfloat16).astype(jnp.float32)
    attended = []
    for p in range(parts):
        copies[parts + p].wait()
        some = slice(p * PART, (p + 1) * PART)
        mixture = jnp.einsum(
            "bhl,bld->bhd", weights[some], value_buf[some], preferred_element_type=jnp.float32
        )
        attended.append(mixture + weights_new[some] * new_value[some])
    attended = jnp.concatenate(attended, axis=0).reshape(rows, heads * head_width)
    attended = attended.astype(jnp.bfloat16)
    attended_ref[...] = attended
    for y in range(ys):
        copies[2 * parts + y].wait()
        out = jnp.dot(attended, weight_buf[y], preferred_element_type=jnp.float32)
        sent_ref[y] = out.astype(sent_ref.dtype)
    for copy in copies[2 * parts + ys :]:
        copy.wait()


def attend(place, lengths, queries, new_keys, new_values, keys, values, out_weight):
    rows, span, head_width = keys.shape[0], keys.shape[2], keys.shape[3]
    ys, width = 4, queries.shape[1]
    scalars = pl.BlockSpec(memory_space=pltpu.SMEM)
    inside = pl.BlockSpec(memory_space=pltpu.VMEM)
    outside = pl.BlockSpec(memory_space=pltpu.HBM)
    return pl.pallas_call(
        attend_kernel,
        in_specs=[scalars] + [outside] * 7,
        out_specs=[inside] * 3,
        out_shape=[
            jax.ShapeDtypeStruct((ys, rows, width), jnp.bfloat16),
            jax.ShapeDtypeStruct((rows, width), jnp.bfloat16),
            jax.ShapeDtypeStruct((ys, width, width), jnp.bfloat16),
        ],
        scratch_shapes=[
            pltpu.SMEM((1, rows), jnp.int32),
            pltpu.VMEM((rows, width), jnp.bfloat16),
            pltpu.VMEM((rows, head_width), jnp.bfloat16),
            pltpu.VMEM((rows, head_width), jnp.bfloat16),
            pltpu.VMEM((rows, span, head_width), jnp.bfloat16),
            pltpu.VMEM((rows, span, head_width), jnp.bfloat16),
            pltpu.VMEM((ys, width, width), jnp.bfloat16),
            pltpu.SemaphoreType.DMA((4 + 2 * rows // PART + 2 * ys,)),
        ],
        compiler_params=pltpu.CompilerParams(vmem_limit_bytes=32 * 2**20),
        cost_estimate=pl.CostEstimate(
            flops=rows * width * width * 8, bytes_accessed=15 * 2**20, transcendentals=0
        ),
        name="attend",
    )(place, *in_hbm(lengths, queries, new_keys, new_values, keys, values, out_weight))


def project_kernel(attended, weight, out_ref):
    for y in range(weight.shape[0]):
        out_ref[y] = jnp.dot(attended[...], weight[y], preferred_element_type=jnp.float32)


def project(attended, weight):
    ys, _, width = weight.shape
    inside = pl.BlockSpec(memory_space=pltpu.VMEM)
    return pl.pallas_call(
        project_kernel,
        in_specs=[inside] * 2,
        out_specs=inside,
        out_shape=jax.ShapeDtypeStruct((ys, attended.shape[0], width), jnp.float32),
        compiler_params=pltpu.CompilerParams(vmem_limit_bytes=16 * 2**20),
        cost_estimate=pl.CostEstimate(
            flops=attended.size * width * 8, bytes_accessed=5 * 2**20, transcendentals=0
        ),
        name="project",
    )(attended, weight)


def gate_up_copies(side, gate, up, target, sems):
    ys, width, units = target.shape[0], target.shape[1], gate.shape[1]
    copies = []
    for y in range(ys):
        rows = pl.ds(pl.multiple_of((2 * y + side) * width, width), width)
        copies.append((gate.at[rows, :], target.at[y, :, pl.ds(0, units)]))
        copies.append((up.at[rows, :], target.at[y, :, pl.ds(units, units)]))
    return [pltpu.make_async_copy(s, t, sems.at[i]) for i, (s, t) in enumerate(copies)]


def load_kernel(core, gate, up, own_weight, sems):
    copies = gate_up_copies(core[0], gate, up, own_weight, sems)
    for copy in copies:
        copy.start()
    for copy in copies:
        copy.wait()


def load_weights(core, gate, up):
    ys, width, units = 4, 768, gate.shape[1]
    inside = pl.BlockSpec(memory_space=pltpu.VMEM)
    outside = pl.BlockSpec(memory_space=pltpu.HBM)
    return pl.pallas_call(
        load_kernel,
        in_specs=[pl.BlockSpec(memory_space=pltpu.SMEM)] + [outside] * 2,
        out_specs=inside,
        out_shape=jax.ShapeDtypeStruct((ys, width, 2 * units), jnp.bfloat16),
        scratch_shapes=[pltpu.SemaphoreType.DMA((2 * ys,))],
        compiler_params=pltpu.CompilerParams(vmem_limit_bytes=16 * 2**20),
        cost_estimate=pl.CostEstimate(flops=0, bytes_accessed=9 * 2**20, transcendentals=0),
        name="load_weights",
    )(core, *in_hbm(gate, up))


def down_copies(side, down, down_other, target, sems):
    ys, width, units = target.shape[0], target.shape[2], down.shape[0]
    copies = []
    for y in range(ys):
        columns = pl.ds(pl.multiple_of((2 * y + side) * width, width), width)
        copies.append((down.at[:, columns], target.at[y, pl.ds(0, units), :]))
        copies.append((down_other.at[:, columns], target.at[y, pl.ds(units, units), :]))
    return [pltpu.make_async_copy(s, t, sems.at[i]) for i, (s, t) in enumerate(copies)]


def add_products(side, source, gain, weight, total, squares):
    ys, zs, xs, cap, width = source.shape
    rows = zs * xs * cap
    flip = FLIP * side
    for y in range(ys):
        parts = [
            source[y ^ flip, z ^ flip, pl.ds(x ^ flip, FLIP)]
            for z in range(zs)
            for x in range(0, xs, FLIP)
        ]
        wide = jnp.concatenate(parts, axis=0).astype(jnp.float32).reshape(rows, width)
        inverse = 1.0 / gain[pl.ds(2 * y + side, 1), :]
        parts = wide * wide * (inverse * inverse)
        step = parts[:, 0:128]
        for j in range(1, width // 128):
            step = step + parts[:, j * 128 : (j + 1) * 128]
        product = jnp.dot(wide.astype(jnp.bfloat16), weight[y], preferred_element_type=jnp.float32)
        if total is None:
            total, squares = product, step
        else:
            total, squares = total + product, squares + step
    return total, squares


def first_kernel(
    core, own, gain, weight, gate, up, down, down_other,
    total_ref, squares_ref, other_weight, out_weight, sems,
):
    copies = gate_up_copies(1 - core[0], gate, up, other_weight, sems.at[0])
    copies += down_copies(core[0], down, down_other, out_weight, sems.at[1])
    for copy in copies:
        copy.start()
    total, squares = add_products(core[0], own, gain, weight, None, None)
    total_ref[...] = total
    squares_ref[...] = squares
    for copy in copies:
        copy.wait()


def second_kernel(core, other, gain, weight, total_ref, squares_ref, hidden_ref):
    ys, width = other.shape[0], other.shape[4]
    total, squares = add_products(
        1 - core[0], other, gain, weight, total_ref[...], squares_ref[...]
    )
    mean = jnp.sum(squares, axis=1, keepdims=True) * (1.0 / (CORES * ys * width))
    total = total * lax.rsqrt(mean + EPSILON)
    units = total.shape[1] // 2
    gate_sum, up_sum = total[:, :units], total[:, units:]
    hidden_ref[...] = (gate_sum / (1.0 + jnp.exp(-gate_sum)) * up_sum).astype(jnp.bfloat16)


def out_kernel(core, hidden, hidden_other, weight, out_ref, buf, sems):
    ys, zs, xs, cap, width = out_ref.shape
    flip = FLIP * core[0]
    both = jnp.concatenate([hidden[...], hidden_other[...]], axis=1)
    copies = []
    for y in range(ys):
        out = jnp.dot(both, weight[y], preferred_element_type=jnp.float32)
        buf[y] = out.reshape(zs, xs, cap, width).astype(buf.dtype)
        for z in range(zs):
            for x in range(0, xs, FLIP):
                copies.append(
                    pltpu.make_async_copy(
                        buf.at[y, z, pl.ds(x, FLIP)],
                        out_ref.at[y ^ flip, z ^ flip, pl.ds(x ^ flip, FLIP)],
                        sems.at[len(copies)],
                    )
                )
                copies[-1].start()
    for copy in copies:
        copy.wait()


def experts_first(core, own, gain, weight, gate, up, down, down_other):
    ys, zs, xs, cap, width = own.shape
    rows, units = zs * xs * cap, down.shape[0]
    inside = pl.BlockSpec(memory_space=pltpu.VMEM)
    outside = pl.BlockSpec(memory_space=pltpu.HBM)
    return pl.pallas_call(
        first_kernel,
        in_specs=[pl.BlockSpec(memory_space=pltpu.SMEM)] + [inside] * 3 + [outside] * 3 + [pl.BlockSpec(memory_space=pl.ANY)],
        out_specs=[inside] * 4,
        out_shape=[
            jax.ShapeDtypeStruct((rows, 2 * units), jnp.float32),
            jax.ShapeDtypeStruct((rows, 128), jnp.float32),
            jax.ShapeDtypeStruct((ys, width, 2 * units), jnp.bfloat16),
            jax.ShapeDtypeStruct((ys, 2 * units, width), jnp.bfloat16),
        ],
        scratch_shapes=[pltpu.SemaphoreType.DMA((2, 2 * ys))],
        compiler_params=pltpu.CompilerParams(vmem_limit_bytes=16 * 2**20),
        cost_estimate=pl.CostEstimate(
            flops=4 * rows * units * ys * width, bytes_accessed=12 * 2**20, transcendentals=0
        ),
        name="experts_first",
    )(core, own, gain, weight, *in_hbm(gate, up, down), down_other)


def experts_second(core, other, gain, weight, total, squares):
    rows, units = total.shape[0], total.shape[1] // 2
    ys, width = weight.shape[0], weight.shape[1]
    inside = pl.BlockSpec(memory_space=pltpu.VMEM)
    return pl.pallas_call(
        second_kernel,
        in_specs=[pl.BlockSpec(memory_space=pltpu.SMEM)] + [inside] * 5,
        out_specs=inside,
        out_shape=jax.ShapeDtypeStruct((rows, units), jnp.bfloat16),
        compiler_params=pltpu.CompilerParams(vmem_limit_bytes=16 * 2**20),
        cost_estimate=pl.CostEstimate(
            flops=4 * rows * units * ys * width, bytes_accessed=12 * 2**20, transcendentals=0
        ),
        name="experts_second",
    )(core, pltpu.with_memory_space_constraint(other, pltpu.VMEM), gain, weight, total, squares)


def experts_out(core, hidden, hidden_other, weight, shape):
    rows, units = hidden.shape
    ys, zs, xs, cap, width = shape
    inside = pl.BlockSpec(memory_space=pltpu.VMEM)
    return pl.pallas_call(
        out_kernel,
        in_specs=[pl.BlockSpec(memory_space=pltpu.SMEM)] + [inside] * 3,
        out_specs=pl.BlockSpec(memory_space=pltpu.HBM),
        out_shape=jax.ShapeDtypeStruct(shape, jnp.bfloat16),
        scratch_shapes=[
            pltpu.VMEM((ys, zs, xs, cap, width), jnp.bfloat16),
            pltpu.SemaphoreType.DMA((ys * zs * xs // FLIP,)),
        ],
        compiler_params=pltpu.CompilerParams(vmem_limit_bytes=20 * 2**20),
        cost_estimate=pl.CostEstimate(
            flops=4 * rows * units * ys * width, bytes_accessed=8 * 2**20, transcendentals=0
        ),
        name="experts_out",
    )(core, hidden, hidden_other, weight)


def swap(value):
    return lax.ppermute(value, "core", [(0, 1), (1, 0)])


def layer_block(
    residual,
    queries,
    new_keys,
    new_values,
    key_cache,
    value_cache,
    cache_lengths,
    out_weight,
    norm_gain,
    gate_weight,
    up_weight,
    down_weight,
    routes,
    route_gates,
):
    rows, width = residual.shape
    ways = lax.axis_size("y") * lax.axis_size("core")
    share = width // ways
    shape = (lax.axis_size("y"), lax.axis_size("z"), lax.axis_size("x"), CAP, share)
    core = lax.axis_index("core")
    column = lax.axis_index("y") * CORES + core

    core_index = core.astype(jnp.int32).reshape(1)
    place = jnp.stack([core, lax.axis_index("y")]).astype(jnp.int32)
    order = jnp.arange(EXPERTS) ^ (FLIP * core)
    start = column * share
    queries, order, start = lax.optimization_barrier((queries, order, start))
    sent, attended, own_columns = attend(
        place, cache_lengths.reshape(1, -1), queries, new_keys, new_values, key_cache, value_cache, out_weight
    )
    kept = project(attended, own_columns)
    first = kept + swap(sent).astype(jnp.float32)
    chips_y = lax.axis_size("y")
    pieces = [
        lax.ppermute(
            first[s].astype(jnp.bfloat16), "y", [(i, (i + s) % chips_y) for i in range(chips_y)]
        )
        for s in range(1, chips_y)
    ]
    gains = norm_gain.reshape(ways, share)
    first, gains, gate_weight, up_weight, down_weight = lax.optimization_barrier(
        (first, gains, gate_weight, up_weight, down_weight)
    )
    down_other = swap(down_weight)
    own_weight = load_weights(core_index, gate_weight, up_weight)
    pieces, own_weight = lax.optimization_barrier((pieces, own_weight))
    middle = lax.dynamic_slice_in_dim(residual, start, share, 1).astype(jnp.float32)
    middle = middle + first[0] + sum(piece.astype(jnp.float32) for piece in pieces)
    gain = lax.dynamic_slice_in_dim(norm_gain, start, share, 0)
    gained = (middle * gain).astype(jnp.bfloat16)

    named = routes[:, :, None] == order[None, None, :]
    coef = jnp.sum(jnp.where(named, route_gates[:, :, None], 0.0), axis=1)
    taken = jnp.any(named, axis=1)
    before = jnp.arange(rows)[:, None] > jnp.arange(rows)[None, :]
    rank = jnp.dot(
        before.astype(jnp.bfloat16), taken.astype(jnp.bfloat16), preferred_element_type=jnp.float32
    )
    match = taken[:, :, None] & (rank.astype(jnp.int32)[:, :, None] == jnp.arange(CAP)[None, None, :])
    chosen = match.astype(jnp.bfloat16).reshape(rows, EXPERTS * CAP)
    blend = jnp.where(match, coef[:, :, None], 0.0).reshape(rows, EXPERTS * CAP)

    outgoing = jnp.einsum("ts,tc->sc", chosen, gained, preferred_element_type=jnp.float32)
    outgoing = outgoing.astype(jnp.bfloat16).reshape(1, EXPERTS, 1, CAP, share)
    own = exchange(jnp.broadcast_to(outgoing, shape))
    other = swap(own)

    total, squares, other_weight, out_weights = experts_first(
        core_index, own, gains, own_weight, gate_weight, up_weight, down_weight, down_other
    )
    hidden = experts_second(core_index, other, gains, other_weight, total, squares)
    outs = experts_out(core_index, hidden, swap(hidden), out_weights, shape)
    returned = exchange(outs)
    merged = jnp.sum(returned.astype(jnp.float32), axis=(0, 2)).reshape(EXPERTS * CAP, share)
    return middle + jnp.dot(blend, merged, precision=lax.Precision.HIGHEST)


def solution(mesh):
    fine = Mesh(mesh.devices.reshape(4, 4, 4, 2), ("z", "x", "y", "core"))
    attn, expert = ("z", "x"), ("y", "core")
    every = attn + expert
    in_specs = (
        P(attn, None),
        P(attn, expert),
        P(attn, expert),
        P(attn, expert),
        P(attn, expert, None, None),
        P(attn, expert, None, None),
        P(attn),
        P(expert, None),
        P(),
        P(None, every),
        P(None, every),
        P(every, None),
        P(attn, None),
        P(attn, None),
    )
    return jax.shard_map(
        layer_block, mesh=fine, in_specs=in_specs, out_specs=P(attn, expert), check_vma=False
    )
```

```python
import functools
import math

import jax
import jax.numpy as jnp
from jax import lax
from jax.experimental import pallas as pl
from jax.experimental.pallas import tpu as pltpu
from jax.sharding import Mesh, PartitionSpec as P

EXPERTS = 4
CAP = 24
CORES = 2
EPSILON = 1e-05

EVERY = ("z", "x", "y", "core")
FLIP = 2
CHIP_ORDERS = [
    [
        (((z ^ (FLIP * c)) * 4 + (x ^ (FLIP * c))) * 4 + (y ^ (FLIP * c))) * CORES + c
        for y in range(4)
        for z in range(4)
        for x in range(4)
    ]
    for c in range(CORES)
]


def exchange(blocks):
    flat = blocks.reshape(64, *blocks.shape[3:])
    flat = lax.all_to_all(
        flat, EVERY, split_axis=0, concat_axis=0, axis_index_groups=CHIP_ORDERS, tiled=True
    )
    return flat.reshape(blocks.shape)


PART = 8


def in_hbm(*arrays):
    return tuple(pltpu.with_memory_space_constraint(array, pltpu.HBM) for array in arrays)


def attend_kernel(
    place, lengths, queries, new_keys, new_values, keys, values, out_weight,
    sent_ref, attended_ref, own_weight,
    length_buf, query_buf, new_key_buf, new_value_buf, key_buf, value_buf, weight_buf, sems,
):
    rows, head_width = new_keys.shape
    heads = queries.shape[1] // head_width
    ys, _, width = weight_buf.shape
    span = keys.shape[2]
    parts = rows // PART
    scale = 1.0 / math.sqrt(head_width)

    copies = [
        (lengths, length_buf),
        (queries, query_buf),
        (new_keys, new_key_buf),
        (new_values, new_value_buf),
    ]
    base = len(copies)
    for cache, target in ((keys, key_buf), (values, value_buf)):
        for p in range(parts):
            some = pl.ds(p * PART, PART)
            copies.append((cache.at[some, 0], target.at[some]))
    for side, target in ((1 - place[0], weight_buf), (place[0], own_weight)):
        for step in range(ys):
            block = 2 * lax.rem(place[1] + step, ys) + side
            columns = pl.ds(pl.multiple_of(block * width, width), width)
            copies.append((out_weight.at[:, columns], target.at[step]))
    copies = [
        pltpu.make_async_copy(source, target, sems.at[i]) for i, (source, target) in enumerate(copies)
    ]
    for copy in copies:
        copy.start()
    for copy in copies[:base]:
        copy.wait()
    copies = copies[base:]

    query_heads = query_buf[...].astype(jnp.float32).reshape(rows, heads, head_width)
    new_key = new_key_buf[...].astype(jnp.float32).reshape(rows, 1, head_width)
    new_value = new_value_buf[...].astype(jnp.float32).reshape(rows, 1, head_width)
    fresh = jnp.sum(query_heads * new_key, axis=2, keepdims=True) * scale
    query_heads = query_heads.astype(jnp.bfloat16)
    position = lax.broadcasted_iota(jnp.int32, (heads, span), 1)
    scores = []
    for p in range(parts):
        copies[p].wait()
        some = slice(p * PART, (p + 1) * PART)
        product = jnp.einsum(
            "bhd,bld->bhl", query_heads[some], key_buf[some], preferred_element_type=jnp.float32
        )
        for i in range(PART):
            visible = position < length_buf[0, p * PART + i]
            scores.append(jnp.where(visible, product[i] * scale, -jnp.inf))
    scores = jnp.stack(scores)
    largest = jnp.maximum(jnp.max(scores, axis=2, keepdims=True), fresh)
    exp_scores = jnp.exp(scores - largest)
    exp_fresh = jnp.exp(fresh - largest)
    inverse = 1.0 / (jnp.sum(exp_scores, axis=2, keepdims=True) + exp_fresh)
    weights = (exp_scores * inverse).astype(jnp.bfloat16)
    weights_new = (exp_fresh * inverse).astype(jnp.bfloat16).astype(jnp.float32)
    attended = []
    for p in range(parts):
        copies[parts + p].wait()
        some = slice(p * PART, (p + 1) * PART)
        mixture = jnp.einsum(
            "bhl,bld->bhd", weights[some], value_buf[some], preferred_element_type=jnp.float32
        )
        attended.append(mixture + weights_new[some] * new_value[some])
    attended = jnp.concatenate(attended, axis=0).reshape(rows, heads * head_width)
    attended = attended.astype(jnp.bfloat16)
    attended_ref[...] = attended
    for y in range(ys):
        copies[2 * parts + y].wait()
        out = jnp.dot(attended, weight_buf[y], preferred_element_type=jnp.float32)
        sent_ref[y] = out.astype(sent_ref.dtype)
    for copy in copies[2 * parts + ys :]:
        copy.wait()


def attend(place, lengths, queries, new_keys, new_values, keys, values, out_weight):
    rows, span, head_width = keys.shape[0], keys.shape[2], keys.shape[3]
    ys, width = 4, queries.shape[1]
    scalars = pl.BlockSpec(memory_space=pltpu.SMEM)
    inside = pl.BlockSpec(memory_space=pltpu.VMEM)
    outside = pl.BlockSpec(memory_space=pltpu.HBM)
    return pl.pallas_call(
        attend_kernel,
        in_specs=[scalars] + [outside] * 7,
        out_specs=[inside] * 3,
        out_shape=[
            jax.ShapeDtypeStruct((ys, rows, width), jnp.bfloat16),
            jax.ShapeDtypeStruct((rows, width), jnp.bfloat16),
            jax.ShapeDtypeStruct((ys, width, width), jnp.bfloat16),
        ],
        scratch_shapes=[
            pltpu.SMEM((1, rows), jnp.int32),
            pltpu.VMEM((rows, width), jnp.bfloat16),
            pltpu.VMEM((rows, head_width), jnp.bfloat16),
            pltpu.VMEM((rows, head_width), jnp.bfloat16),
            pltpu.VMEM((rows, span, head_width), jnp.bfloat16),
            pltpu.VMEM((rows, span, head_width), jnp.bfloat16),
            pltpu.VMEM((ys, width, width), jnp.bfloat16),
            pltpu.SemaphoreType.DMA((4 + 2 * rows // PART + 2 * ys,)),
        ],
        compiler_params=pltpu.CompilerParams(vmem_limit_bytes=32 * 2**20),
        cost_estimate=pl.CostEstimate(
            flops=rows * width * width * 8, bytes_accessed=15 * 2**20, transcendentals=0
        ),
        name="attend",
    )(place, *in_hbm(lengths, queries, new_keys, new_values, keys, values, out_weight))


def project_kernel(attended, weight, out_ref):
    for y in range(weight.shape[0]):
        out_ref[y] = jnp.dot(attended[...], weight[y], preferred_element_type=jnp.float32)


def project(attended, weight):
    ys, _, width = weight.shape
    inside = pl.BlockSpec(memory_space=pltpu.VMEM)
    return pl.pallas_call(
        project_kernel,
        in_specs=[inside] * 2,
        out_specs=inside,
        out_shape=jax.ShapeDtypeStruct((ys, attended.shape[0], width), jnp.float32),
        compiler_params=pltpu.CompilerParams(vmem_limit_bytes=16 * 2**20),
        cost_estimate=pl.CostEstimate(
            flops=attended.size * width * 8, bytes_accessed=5 * 2**20, transcendentals=0
        ),
        name="project",
    )(attended, weight)


def gate_up_copies(side, gate, up, target, sems):
    ys, width, units = target.shape[0], target.shape[1], gate.shape[1]
    copies = []
    for y in range(ys):
        rows = pl.ds(pl.multiple_of((2 * y + side) * width, width), width)
        copies.append((gate.at[rows, :], target.at[y, :, pl.ds(0, units)]))
        copies.append((up.at[rows, :], target.at[y, :, pl.ds(units, units)]))
    return [pltpu.make_async_copy(s, t, sems.at[i]) for i, (s, t) in enumerate(copies)]


def load_kernel(core, gate, up, own_weight, sems):
    copies = gate_up_copies(core[0], gate, up, own_weight, sems)
    for copy in copies:
        copy.start()
    for copy in copies:
        copy.wait()


def load_weights(core, gate, up):
    ys, width, units = 4, 768, gate.shape[1]
    inside = pl.BlockSpec(memory_space=pltpu.VMEM)
    outside = pl.BlockSpec(memory_space=pltpu.HBM)
    return pl.pallas_call(
        load_kernel,
        in_specs=[pl.BlockSpec(memory_space=pltpu.SMEM)] + [outside] * 2,
        out_specs=inside,
        out_shape=jax.ShapeDtypeStruct((ys, width, 2 * units), jnp.bfloat16),
        scratch_shapes=[pltpu.SemaphoreType.DMA((2 * ys,))],
        compiler_params=pltpu.CompilerParams(vmem_limit_bytes=16 * 2**20),
        cost_estimate=pl.CostEstimate(flops=0, bytes_accessed=9 * 2**20, transcendentals=0),
        name="load_weights",
    )(core, *in_hbm(gate, up))


def down_copies(side, down, down_other, target, sems):
    ys, width, units = target.shape[0], target.shape[2], down.shape[0]
    copies = []
    for y in range(ys):
        columns = pl.ds(pl.multiple_of((2 * y + side) * width, width), width)
        copies.append((down.at[:, columns], target.at[y, pl.ds(0, units), :]))
        copies.append((down_other.at[:, columns], target.at[y, pl.ds(units, units), :]))
    return [pltpu.make_async_copy(s, t, sems.at[i]) for i, (s, t) in enumerate(copies)]


def add_products(side, source, gain, weight, total, squares):
    ys, zs, xs, cap, width = source.shape
    rows = zs * xs * cap
    flip = FLIP * side
    for y in range(ys):
        parts = [
            source[y ^ flip, z ^ flip, pl.ds(x ^ flip, FLIP)]
            for z in range(zs)
            for x in range(0, xs, FLIP)
        ]
        wide = jnp.concatenate(parts, axis=0).astype(jnp.float32).reshape(rows, width)
        inverse = 1.0 / gain[pl.ds(2 * y + side, 1), :]
        parts = wide * wide * (inverse * inverse)
        step = parts[:, 0:128]
        for j in range(1, width // 128):
            step = step + parts[:, j * 128 : (j + 1) * 128]
        product = jnp.dot(wide.astype(jnp.bfloat16), weight[y], preferred_element_type=jnp.float32)
        if total is None:
            total, squares = product, step
        else:
            total, squares = total + product, squares + step
    return total, squares


def first_kernel(
    core, own, gain, weight, gate, up, down, down_other,
    total_ref, squares_ref, other_weight, out_weight, sems,
):
    copies = gate_up_copies(1 - core[0], gate, up, other_weight, sems.at[0])
    copies += down_copies(core[0], down, down_other, out_weight, sems.at[1])
    for copy in copies:
        copy.start()
    total, squares = add_products(core[0], own, gain, weight, None, None)
    total_ref[...] = total
    squares_ref[...] = squares
    for copy in copies:
        copy.wait()


def second_kernel(core, other, gain, weight, total_ref, squares_ref, hidden_ref):
    ys, width = other.shape[0], other.shape[4]
    total, squares = add_products(
        1 - core[0], other, gain, weight, total_ref[...], squares_ref[...]
    )
    mean = jnp.sum(squares, axis=1, keepdims=True) * (1.0 / (CORES * ys * width))
    total = total * lax.rsqrt(mean + EPSILON)
    units = total.shape[1] // 2
    gate_sum, up_sum = total[:, :units], total[:, units:]
    hidden_ref[...] = (gate_sum / (1.0 + jnp.exp(-gate_sum)) * up_sum).astype(jnp.bfloat16)


def out_kernel(core, hidden, hidden_other, weight, out_ref, buf, sems):
    ys, zs, xs, cap, width = out_ref.shape
    flip = FLIP * core[0]
    both = jnp.concatenate([hidden[...], hidden_other[...]], axis=1)
    copies = []
    for y in range(ys):
        out = jnp.dot(both, weight[y], preferred_element_type=jnp.float32)
        buf[y] = out.reshape(zs, xs, cap, width).astype(buf.dtype)
        for z in range(zs):
            for x in range(0, xs, FLIP):
                copies.append(
                    pltpu.make_async_copy(
                        buf.at[y, z, pl.ds(x, FLIP)],
                        out_ref.at[y ^ flip, z ^ flip, pl.ds(x ^ flip, FLIP)],
                        sems.at[len(copies)],
                    )
                )
                copies[-1].start()
    for copy in copies:
        copy.wait()


def experts_first(core, own, gain, weight, gate, up, down, down_other):
    ys, zs, xs, cap, width = own.shape
    rows, units = zs * xs * cap, down.shape[0]
    inside = pl.BlockSpec(memory_space=pltpu.VMEM)
    outside = pl.BlockSpec(memory_space=pltpu.HBM)
    return pl.pallas_call(
        first_kernel,
        in_specs=[pl.BlockSpec(memory_space=pltpu.SMEM)] + [inside] * 3 + [outside] * 3 + [pl.BlockSpec(memory_space=pl.ANY)],
        out_specs=[inside] * 4,
        out_shape=[
            jax.ShapeDtypeStruct((rows, 2 * units), jnp.float32),
            jax.ShapeDtypeStruct((rows, 128), jnp.float32),
            jax.ShapeDtypeStruct((ys, width, 2 * units), jnp.bfloat16),
            jax.ShapeDtypeStruct((ys, 2 * units, width), jnp.bfloat16),
        ],
        scratch_shapes=[pltpu.SemaphoreType.DMA((2, 2 * ys))],
        compiler_params=pltpu.CompilerParams(vmem_limit_bytes=16 * 2**20),
        cost_estimate=pl.CostEstimate(
            flops=4 * rows * units * ys * width, bytes_accessed=12 * 2**20, transcendentals=0
        ),
        name="experts_first",
    )(core, own, gain, weight, *in_hbm(gate, up, down), down_other)


def experts_second(core, other, gain, weight, total, squares):
    rows, units = total.shape[0], total.shape[1] // 2
    ys, width = weight.shape[0], weight.shape[1]
    inside = pl.BlockSpec(memory_space=pltpu.VMEM)
    return pl.pallas_call(
        second_kernel,
        in_specs=[pl.BlockSpec(memory_space=pltpu.SMEM)] + [inside] * 5,
        out_specs=inside,
        out_shape=jax.ShapeDtypeStruct((rows, units), jnp.bfloat16),
        compiler_params=pltpu.CompilerParams(vmem_limit_bytes=16 * 2**20),
        cost_estimate=pl.CostEstimate(
            flops=4 * rows * units * ys * width, bytes_accessed=12 * 2**20, transcendentals=0
        ),
        name="experts_second",
    )(core, pltpu.with_memory_space_constraint(other, pltpu.VMEM), gain, weight, total, squares)


def experts_out(core, hidden, hidden_other, weight, shape):
    rows, units = hidden.shape
    ys, zs, xs, cap, width = shape
    inside = pl.BlockSpec(memory_space=pltpu.VMEM)
    return pl.pallas_call(
        out_kernel,
        in_specs=[pl.BlockSpec(memory_space=pltpu.SMEM)] + [inside] * 3,
        out_specs=pl.BlockSpec(memory_space=pltpu.HBM),
        out_shape=jax.ShapeDtypeStruct(shape, jnp.bfloat16),
        scratch_shapes=[
            pltpu.VMEM((ys, zs, xs, cap, width), jnp.bfloat16),
            pltpu.SemaphoreType.DMA((ys * zs * xs // FLIP,)),
        ],
        compiler_params=pltpu.CompilerParams(vmem_limit_bytes=20 * 2**20),
        cost_estimate=pl.CostEstimate(
            flops=4 * rows * units * ys * width, bytes_accessed=8 * 2**20, transcendentals=0
        ),
        name="experts_out",
    )(core, hidden, hidden_other, weight)


def swap(value):
    return lax.ppermute(value, "core", [(0, 1), (1, 0)])


def layer_block(
    residual,
    queries,
    new_keys,
    new_values,
    key_cache,
    value_cache,
    cache_lengths,
    out_weight,
    norm_gain,
    gate_weight,
    up_weight,
    down_weight,
    routes,
    route_gates,
):
    rows, width = residual.shape
    ways = lax.axis_size("y") * lax.axis_size("core")
    share = width // ways
    shape = (lax.axis_size("y"), lax.axis_size("z"), lax.axis_size("x"), CAP, share)
    core = lax.axis_index("core")
    column = lax.axis_index("y") * CORES + core

    core_index = core.astype(jnp.int32).reshape(1)
    place = jnp.stack([core, lax.axis_index("y")]).astype(jnp.int32)
    order = jnp.arange(EXPERTS) ^ (FLIP * core)
    start = (column * share).astype(jnp.uint32)
    queries, order, start = lax.optimization_barrier((queries, order, start))
    sent, attended, own_columns = attend(
        place, cache_lengths.reshape(1, -1), queries, new_keys, new_values, key_cache, value_cache, out_weight
    )
    kept, mine = lax.optimization_barrier(
        (
            project(attended, own_columns),
            lax.dynamic_slice(residual, (jnp.uint32(0), start), (rows, share)),
        )
    )
    first = kept + swap(sent).astype(jnp.float32)
    chips_y = lax.axis_size("y")
    pieces = [
        lax.ppermute(
            first[s].astype(jnp.bfloat16), "y", [(i, (i + s) % chips_y) for i in range(chips_y)]
        )
        for s in range(1, chips_y)
    ]
    gains = norm_gain.reshape(ways, share)
    first, gains, gate_weight, up_weight, down_weight = lax.optimization_barrier(
        (first, gains, gate_weight, up_weight, down_weight)
    )
    down_other = swap(down_weight)
    own_weight = load_weights(core_index, gate_weight, up_weight)
    pieces, own_weight = lax.optimization_barrier((pieces, own_weight))
    middle = mine.astype(jnp.float32) + first[0] + sum(piece.astype(jnp.float32) for piece in pieces)
    gain = lax.dynamic_slice(norm_gain, (start,), (share,))
    gained = (middle * gain).astype(jnp.bfloat16)

    named = routes[:, :, None] == order[None, None, :]
    coef = jnp.sum(jnp.where(named, route_gates[:, :, None], 0.0), axis=1)
    taken = jnp.any(named, axis=1)
    before = jnp.arange(rows)[:, None] > jnp.arange(rows)[None, :]
    rank = jnp.dot(
        before.astype(jnp.bfloat16), taken.astype(jnp.bfloat16), preferred_element_type=jnp.float32
    )
    match = taken[:, :, None] & (rank.astype(jnp.int32)[:, :, None] == jnp.arange(CAP)[None, None, :])
    chosen = match.astype(jnp.bfloat16).reshape(rows, EXPERTS * CAP)
    blend = jnp.where(match, coef[:, :, None], 0.0).reshape(rows, EXPERTS * CAP)

    outgoing = jnp.einsum("ts,tc->sc", chosen, gained, preferred_element_type=jnp.float32)
    outgoing = outgoing.astype(jnp.bfloat16).reshape(1, EXPERTS, 1, CAP, share)
    own = exchange(jnp.broadcast_to(outgoing, shape))
    other = swap(own)

    total, squares, other_weight, out_weights = experts_first(
        core_index, own, gains, own_weight, gate_weight, up_weight, down_weight, down_other
    )
    hidden = experts_second(core_index, other, gains, other_weight, total, squares)
    outs = experts_out(core_index, hidden, swap(hidden), out_weights, shape)
    returned = exchange(outs)
    merged = jnp.sum(returned.astype(jnp.float32), axis=(0, 2)).reshape(EXPERTS * CAP, share)
    return middle + jnp.dot(blend, merged, precision=lax.Precision.HIGH)


def solution(mesh):
    fine = Mesh(mesh.devices.reshape(4, 4, 4, 2), ("z", "x", "y", "core"))
    attn, expert = ("z", "x"), ("y", "core")
    every = attn + expert
    in_specs = (
        P(attn, None),
        P(attn, expert),
        P(attn, expert),
        P(attn, expert),
        P(attn, expert, None, None),
        P(attn, expert, None, None),
        P(attn),
        P(expert, None),
        P(),
        P(None, every),
        P(None, every),
        P(every, None),
        P(attn, None),
        P(attn, None),
    )
    return jax.shard_map(
        layer_block, mesh=fine, in_specs=in_specs, out_specs=P(attn, expert), check_vma=False
    )
```

```python
import functools
import math

import jax
import jax.numpy as jnp
from jax import lax
from jax.experimental import pallas as pl
from jax.experimental.pallas import tpu as pltpu
from jax.sharding import Mesh, PartitionSpec as P

EXPERTS = 4
CAP = 24
CORES = 2
EPSILON = 1e-05

EVERY = ("z", "x", "y", "core")
FLIP = 2
CHIP_ORDERS = [
    [
        (((z ^ (FLIP * c)) * 4 + (x ^ (FLIP * c))) * 4 + (y ^ (FLIP * c))) * CORES + c
        for y in range(4)
        for z in range(4)
        for x in range(4)
    ]
    for c in range(CORES)
]


def exchange(blocks):
    flat = blocks.reshape(64, *blocks.shape[3:])
    flat = lax.all_to_all(
        flat, EVERY, split_axis=0, concat_axis=0, axis_index_groups=CHIP_ORDERS, tiled=True
    )
    return flat.reshape(blocks.shape)


PART = 8


def in_hbm(*arrays):
    return tuple(pltpu.with_memory_space_constraint(array, pltpu.HBM) for array in arrays)


def attend_kernel(
    place, lengths, queries, new_keys, new_values, keys, values, out_weight,
    sent_ref, attended_ref, own_weight,
    length_buf, query_buf, new_key_buf, new_value_buf, key_buf, value_buf, weight_buf, sems,
):
    rows, head_width = new_keys.shape
    heads = queries.shape[1] // head_width
    ys, _, width = weight_buf.shape
    span = keys.shape[2]
    parts = rows // PART
    scale = 1.0 / math.sqrt(head_width)

    copies = [
        (lengths, length_buf),
        (queries, query_buf),
        (new_keys, new_key_buf),
        (new_values, new_value_buf),
    ]
    base = len(copies)
    for cache, target in ((keys, key_buf), (values, value_buf)):
        for p in range(parts):
            some = pl.ds(p * PART, PART)
            copies.append((cache.at[some, 0], target.at[some]))
    for side, target in ((1 - place[0], weight_buf), (place[0], own_weight)):
        for step in range(ys):
            block = 2 * lax.rem(place[1] + step, ys) + side
            columns = pl.ds(pl.multiple_of(block * width, width), width)
            copies.append((out_weight.at[:, columns], target.at[step]))
    copies = [
        pltpu.make_async_copy(source, target, sems.at[i]) for i, (source, target) in enumerate(copies)
    ]
    for copy in copies:
        copy.start()
    for copy in copies[:base]:
        copy.wait()
    copies = copies[base:]

    query_heads = query_buf[...].astype(jnp.float32).reshape(rows, heads, head_width)
    new_key = new_key_buf[...].astype(jnp.float32).reshape(rows, 1, head_width)
    new_value = new_value_buf[...].astype(jnp.float32).reshape(rows, 1, head_width)
    fresh = jnp.sum(query_heads * new_key, axis=2, keepdims=True) * scale
    query_heads = query_heads.astype(jnp.bfloat16)
    position = lax.broadcasted_iota(jnp.int32, (heads, span), 1)
    scores = []
    for p in range(parts):
        copies[p].wait()
        some = slice(p * PART, (p + 1) * PART)
        product = jnp.einsum(
            "bhd,bld->bhl", query_heads[some], key_buf[some], preferred_element_type=jnp.float32
        )
        for i in range(PART):
            visible = position < length_buf[0, p * PART + i]
            scores.append(jnp.where(visible, product[i] * scale, -jnp.inf))
    scores = jnp.stack(scores)
    largest = jnp.maximum(jnp.max(scores, axis=2, keepdims=True), fresh)
    exp_scores = jnp.exp(scores - largest)
    exp_fresh = jnp.exp(fresh - largest)
    inverse = 1.0 / (jnp.sum(exp_scores, axis=2, keepdims=True) + exp_fresh)
    weights = (exp_scores * inverse).astype(jnp.bfloat16)
    weights_new = (exp_fresh * inverse).astype(jnp.bfloat16).astype(jnp.float32)
    attended = []
    for p in range(parts):
        copies[parts + p].wait()
        some = slice(p * PART, (p + 1) * PART)
        mixture = jnp.einsum(
            "bhl,bld->bhd", weights[some], value_buf[some], preferred_element_type=jnp.float32
        )
        attended.append(mixture + weights_new[some] * new_value[some])
    attended = jnp.concatenate(attended, axis=0).reshape(rows, heads * head_width)
    attended = attended.astype(jnp.bfloat16)
    attended_ref[...] = attended
    for y in range(ys):
        copies[2 * parts + y].wait()
        out = jnp.dot(attended, weight_buf[y], preferred_element_type=jnp.float32)
        sent_ref[y] = out.astype(sent_ref.dtype)
    for copy in copies[2 * parts + ys :]:
        copy.wait()


def attend(place, lengths, queries, new_keys, new_values, keys, values, out_weight):
    rows, span, head_width = keys.shape[0], keys.shape[2], keys.shape[3]
    ys, width = 4, queries.shape[1]
    scalars = pl.BlockSpec(memory_space=pltpu.SMEM)
    inside = pl.BlockSpec(memory_space=pltpu.VMEM)
    outside = pl.BlockSpec(memory_space=pltpu.HBM)
    return pl.pallas_call(
        attend_kernel,
        in_specs=[scalars] + [outside] * 7,
        out_specs=[inside] * 3,
        out_shape=[
            jax.ShapeDtypeStruct((ys, rows, width), jnp.bfloat16),
            jax.ShapeDtypeStruct((rows, width), jnp.bfloat16),
            jax.ShapeDtypeStruct((ys, width, width), jnp.bfloat16),
        ],
        scratch_shapes=[
            pltpu.SMEM((1, rows), jnp.int32),
            pltpu.VMEM((rows, width), jnp.bfloat16),
            pltpu.VMEM((rows, head_width), jnp.bfloat16),
            pltpu.VMEM((rows, head_width), jnp.bfloat16),
            pltpu.VMEM((rows, span, head_width), jnp.bfloat16),
            pltpu.VMEM((rows, span, head_width), jnp.bfloat16),
            pltpu.VMEM((ys, width, width), jnp.bfloat16),
            pltpu.SemaphoreType.DMA((4 + 2 * rows // PART + 2 * ys,)),
        ],
        compiler_params=pltpu.CompilerParams(vmem_limit_bytes=32 * 2**20),
        cost_estimate=pl.CostEstimate(
            flops=rows * width * width * 8, bytes_accessed=15 * 2**20, transcendentals=0
        ),
        name="attend",
    )(place, *in_hbm(lengths, queries, new_keys, new_values, keys, values, out_weight))


def project_kernel(attended, weight, out_ref):
    for y in range(weight.shape[0]):
        out_ref[y] = jnp.dot(attended[...], weight[y], preferred_element_type=jnp.float32)


def project(attended, weight):
    ys, _, width = weight.shape
    inside = pl.BlockSpec(memory_space=pltpu.VMEM)
    return pl.pallas_call(
        project_kernel,
        in_specs=[inside] * 2,
        out_specs=inside,
        out_shape=jax.ShapeDtypeStruct((ys, attended.shape[0], width), jnp.float32),
        compiler_params=pltpu.CompilerParams(vmem_limit_bytes=16 * 2**20),
        cost_estimate=pl.CostEstimate(
            flops=attended.size * width * 8, bytes_accessed=5 * 2**20, transcendentals=0
        ),
        name="project",
    )(attended, weight)


def gate_up_copies(side, gate, up, target, sems):
    ys, width, units = target.shape[0], target.shape[1], gate.shape[1]
    copies = []
    for y in range(ys):
        rows = pl.ds(pl.multiple_of((2 * y + side) * width, width), width)
        copies.append((gate.at[rows, :], target.at[y, :, pl.ds(0, units)]))
        copies.append((up.at[rows, :], target.at[y, :, pl.ds(units, units)]))
    return [pltpu.make_async_copy(s, t, sems.at[i]) for i, (s, t) in enumerate(copies)]


def load_kernel(core, gate, up, own_weight, sems):
    copies = gate_up_copies(core[0], gate, up, own_weight, sems)
    for copy in copies:
        copy.start()
    for copy in copies:
        copy.wait()


def load_weights(core, gate, up):
    ys, width, units = 4, 768, gate.shape[1]
    inside = pl.BlockSpec(memory_space=pltpu.VMEM)
    outside = pl.BlockSpec(memory_space=pltpu.HBM)
    return pl.pallas_call(
        load_kernel,
        in_specs=[pl.BlockSpec(memory_space=pltpu.SMEM)] + [outside] * 2,
        out_specs=inside,
        out_shape=jax.ShapeDtypeStruct((ys, width, 2 * units), jnp.bfloat16),
        scratch_shapes=[pltpu.SemaphoreType.DMA((2 * ys,))],
        compiler_params=pltpu.CompilerParams(vmem_limit_bytes=16 * 2**20),
        cost_estimate=pl.CostEstimate(flops=0, bytes_accessed=9 * 2**20, transcendentals=0),
        name="load_weights",
    )(core, *in_hbm(gate, up))


def down_copies(side, down, down_other, target, sems):
    ys, width, units = target.shape[0], target.shape[2], down.shape[0]
    copies = []
    for y in range(ys):
        columns = pl.ds(pl.multiple_of((2 * y + side) * width, width), width)
        copies.append((down.at[:, columns], target.at[y, pl.ds(0, units), :]))
        copies.append((down_other.at[:, columns], target.at[y, pl.ds(units, units), :]))
    return [pltpu.make_async_copy(s, t, sems.at[i]) for i, (s, t) in enumerate(copies)]


def add_products(side, source, gain, weight, total, squares):
    ys, zs, xs, cap, width = source.shape
    rows = zs * xs * cap
    flip = FLIP * side
    for y in range(ys):
        parts = [
            source[y ^ flip, z ^ flip, pl.ds(x ^ flip, FLIP)]
            for z in range(zs)
            for x in range(0, xs, FLIP)
        ]
        wide = jnp.concatenate(parts, axis=0).astype(jnp.float32).reshape(rows, width)
        inverse = 1.0 / gain[pl.ds(2 * y + side, 1), :]
        parts = wide * wide * (inverse * inverse)
        step = parts[:, 0:128]
        for j in range(1, width // 128):
            step = step + parts[:, j * 128 : (j + 1) * 128]
        product = jnp.dot(wide.astype(jnp.bfloat16), weight[y], preferred_element_type=jnp.float32)
        if total is None:
            total, squares = product, step
        else:
            total, squares = total + product, squares + step
    return total, squares


def first_kernel(
    core, own, gain, weight, gate, up, down, down_other,
    total_ref, squares_ref, other_weight, out_weight, sems,
):
    copies = gate_up_copies(1 - core[0], gate, up, other_weight, sems.at[0])
    copies += down_copies(core[0], down, down_other, out_weight, sems.at[1])
    for copy in copies:
        copy.start()
    total, squares = add_products(core[0], own, gain, weight, None, None)
    total_ref[...] = total
    squares_ref[...] = squares
    for copy in copies:
        copy.wait()


def second_kernel(core, other, gain, weight, total_ref, squares_ref, hidden_ref):
    ys, width = other.shape[0], other.shape[4]
    total, squares = add_products(
        1 - core[0], other, gain, weight, total_ref[...], squares_ref[...]
    )
    mean = jnp.sum(squares, axis=1, keepdims=True) * (1.0 / (CORES * ys * width))
    total = total * lax.rsqrt(mean + EPSILON)
    units = total.shape[1] // 2
    gate_sum, up_sum = total[:, :units], total[:, units:]
    hidden_ref[...] = (gate_sum / (1.0 + jnp.exp(-gate_sum)) * up_sum).astype(jnp.bfloat16)


def out_kernel(core, hidden, hidden_other, weight, out_ref, buf, sems):
    ys, zs, xs, cap, width = out_ref.shape
    flip = FLIP * core[0]
    both = jnp.concatenate([hidden[...], hidden_other[...]], axis=1)
    copies = []
    for y in range(ys):
        out = jnp.dot(both, weight[y], preferred_element_type=jnp.float32)
        buf[y] = out.reshape(zs, xs, cap, width).astype(buf.dtype)
        for z in range(zs):
            for x in range(0, xs, FLIP):
                copies.append(
                    pltpu.make_async_copy(
                        buf.at[y, z, pl.ds(x, FLIP)],
                        out_ref.at[y ^ flip, z ^ flip, pl.ds(x ^ flip, FLIP)],
                        sems.at[len(copies)],
                    )
                )
                copies[-1].start()
    for copy in copies:
        copy.wait()


def experts_first(core, own, gain, weight, gate, up, down, down_other):
    ys, zs, xs, cap, width = own.shape
    rows, units = zs * xs * cap, down.shape[0]
    inside = pl.BlockSpec(memory_space=pltpu.VMEM)
    outside = pl.BlockSpec(memory_space=pltpu.HBM)
    return pl.pallas_call(
        first_kernel,
        in_specs=[pl.BlockSpec(memory_space=pltpu.SMEM)] + [inside] * 3 + [outside] * 3 + [pl.BlockSpec(memory_space=pl.ANY)],
        out_specs=[inside] * 4,
        out_shape=[
            jax.ShapeDtypeStruct((rows, 2 * units), jnp.float32),
            jax.ShapeDtypeStruct((rows, 128), jnp.float32),
            jax.ShapeDtypeStruct((ys, width, 2 * units), jnp.bfloat16),
            jax.ShapeDtypeStruct((ys, 2 * units, width), jnp.bfloat16),
        ],
        scratch_shapes=[pltpu.SemaphoreType.DMA((2, 2 * ys))],
        compiler_params=pltpu.CompilerParams(vmem_limit_bytes=16 * 2**20),
        cost_estimate=pl.CostEstimate(
            flops=4 * rows * units * ys * width, bytes_accessed=12 * 2**20, transcendentals=0
        ),
        name="experts_first",
    )(core, own, gain, weight, *in_hbm(gate, up, down), down_other)


def experts_second(core, other, gain, weight, total, squares):
    rows, units = total.shape[0], total.shape[1] // 2
    ys, width = weight.shape[0], weight.shape[1]
    inside = pl.BlockSpec(memory_space=pltpu.VMEM)
    return pl.pallas_call(
        second_kernel,
        in_specs=[pl.BlockSpec(memory_space=pltpu.SMEM)] + [inside] * 5,
        out_specs=inside,
        out_shape=jax.ShapeDtypeStruct((rows, units), jnp.bfloat16),
        compiler_params=pltpu.CompilerParams(vmem_limit_bytes=16 * 2**20),
        cost_estimate=pl.CostEstimate(
            flops=4 * rows * units * ys * width, bytes_accessed=12 * 2**20, transcendentals=0
        ),
        name="experts_second",
    )(core, pltpu.with_memory_space_constraint(other, pltpu.VMEM), gain, weight, total, squares)


def experts_out(core, hidden, hidden_other, weight, shape):
    rows, units = hidden.shape
    ys, zs, xs, cap, width = shape
    inside = pl.BlockSpec(memory_space=pltpu.VMEM)
    return pl.pallas_call(
        out_kernel,
        in_specs=[pl.BlockSpec(memory_space=pltpu.SMEM)] + [inside] * 3,
        out_specs=pl.BlockSpec(memory_space=pltpu.HBM),
        out_shape=jax.ShapeDtypeStruct(shape, jnp.bfloat16),
        scratch_shapes=[
            pltpu.VMEM((ys, zs, xs, cap, width), jnp.bfloat16),
            pltpu.SemaphoreType.DMA((ys * zs * xs // FLIP,)),
        ],
        compiler_params=pltpu.CompilerParams(vmem_limit_bytes=20 * 2**20),
        cost_estimate=pl.CostEstimate(
            flops=4 * rows * units * ys * width, bytes_accessed=8 * 2**20, transcendentals=0
        ),
        name="experts_out",
    )(core, hidden, hidden_other, weight)


def swap(value):
    return lax.ppermute(value, "core", [(0, 1), (1, 0)])


def layer_block(
    residual,
    queries,
    new_keys,
    new_values,
    key_cache,
    value_cache,
    cache_lengths,
    out_weight,
    norm_gain,
    gate_weight,
    up_weight,
    down_weight,
    routes,
    route_gates,
):
    rows, width = residual.shape
    ways = lax.axis_size("y") * lax.axis_size("core")
    share = width // ways
    shape = (lax.axis_size("y"), lax.axis_size("z"), lax.axis_size("x"), CAP, share)
    core = lax.axis_index("core")
    column = lax.axis_index("y") * CORES + core

    core_index = core.astype(jnp.int32).reshape(1)
    place = jnp.stack([core, lax.axis_index("y")]).astype(jnp.int32)
    order = jnp.arange(EXPERTS) ^ (FLIP * core)
    start = (column * share).astype(jnp.uint32)
    queries, order, start = lax.optimization_barrier((queries, order, start))
    sent, attended, own_columns = attend(
        place, cache_lengths.reshape(1, -1), queries, new_keys, new_values, key_cache, value_cache, out_weight
    )
    kept, mine = lax.optimization_barrier(
        (
            project(attended, own_columns),
            lax.dynamic_slice(residual, (jnp.uint32(0), start), (rows, share)),
        )
    )
    first = kept + swap(sent).astype(jnp.float32)
    chips_y = lax.axis_size("y")
    pieces = [
        lax.ppermute(
            first[s].astype(jnp.bfloat16), "y", [(i, (i + s) % chips_y) for i in range(chips_y)]
        )
        for s in (1, 3, 2)
    ]
    gains = norm_gain.reshape(ways, share)
    first, gains, gate_weight, up_weight, down_weight = lax.optimization_barrier(
        (first, gains, gate_weight, up_weight, down_weight)
    )
    down_other = swap(down_weight)
    own_weight = load_weights(core_index, gate_weight, up_weight)
    pieces, own_weight = lax.optimization_barrier((pieces, own_weight))
    middle = mine.astype(jnp.float32) + first[0] + sum(piece.astype(jnp.float32) for piece in pieces)
    gain = lax.dynamic_slice(norm_gain, (start,), (share,))
    gained = (middle * gain).astype(jnp.bfloat16)

    named = routes[:, :, None] == order[None, None, :]
    coef = jnp.sum(jnp.where(named, route_gates[:, :, None], 0.0), axis=1)
    taken = jnp.any(named, axis=1)
    before = jnp.arange(rows)[:, None] > jnp.arange(rows)[None, :]
    rank = jnp.dot(
        before.astype(jnp.bfloat16), taken.astype(jnp.bfloat16), preferred_element_type=jnp.float32
    )
    match = taken[:, :, None] & (rank.astype(jnp.int32)[:, :, None] == jnp.arange(CAP)[None, None, :])
    chosen = match.astype(jnp.bfloat16).reshape(rows, EXPERTS * CAP)
    blend = jnp.where(match, coef[:, :, None], 0.0).reshape(rows, EXPERTS * CAP)

    outgoing = jnp.einsum("ts,tc->sc", chosen, gained, preferred_element_type=jnp.float32)
    outgoing = outgoing.astype(jnp.bfloat16).reshape(1, EXPERTS, 1, CAP, share)
    own = exchange(jnp.broadcast_to(outgoing, shape))
    other = swap(own)

    total, squares, other_weight, out_weights = experts_first(
        core_index, own, gains, own_weight, gate_weight, up_weight, down_weight, down_other
    )
    hidden = experts_second(core_index, other, gains, other_weight, total, squares)
    outs = experts_out(core_index, hidden, swap(hidden), out_weights, shape)
    returned = exchange(outs)
    merged = jnp.sum(returned.astype(jnp.float32), axis=(0, 2)).reshape(EXPERTS * CAP, share)
    return middle + jnp.dot(blend, merged, precision=lax.Precision.HIGH)


def solution(mesh):
    fine = Mesh(mesh.devices.reshape(4, 4, 4, 2), ("z", "x", "y", "core"))
    attn, expert = ("z", "x"), ("y", "core")
    every = attn + expert
    in_specs = (
        P(attn, None),
        P(attn, expert),
        P(attn, expert),
        P(attn, expert),
        P(attn, expert, None, None),
        P(attn, expert, None, None),
        P(attn),
        P(expert, None),
        P(),
        P(None, every),
        P(None, every),
        P(every, None),
        P(attn, None),
        P(attn, None),
    )
    return jax.shard_map(
        layer_block, mesh=fine, in_specs=in_specs, out_specs=P(attn, expert), check_vma=False
    )
```
